256 devices in a mesh: leaf: 64 (over y, z, core), vec: 4 (over x).
Axes of the slice: x: 4, y: 4, z: 8, core: 2. Of those that a mesh axis runs over, the one named last changes fastest.
Arguments:
- points_x: float32 [16, 262144], P('vec', 'leaf'), may hold values from -6 to 6
- near_list: int32 [4096, 8], P('leaf'), may hold values from 0 to 4095, as said below
- near_blocks: float32 [8, 64, 262144], P('vec', None, 'leaf'), may hold values from -0.25 to 0.25
- leaf_basis: float32 [32, 262144], P(None, 'leaf'), may hold values from -0.75 to 0.75
- out_basis: float32 [32, 262144], P(None, 'leaf'), may hold values from -1 to 1
- up_transfer: float32 [32, 131072], P(None, 'leaf'), may hold values from -0.375 to 0.375
- down_transfer: float32 [32, 131072], P(None, 'leaf'), may hold values from -1 to 1
- send_leaves: int32 [64, 64, 8], P('leaf'), may hold values from 0 to 63, as said below
- send_counts: int32 [64, 64], P('leaf'), may hold values from 1 to 8, as said below
- recv_slot: int32 [4096, 16], P('leaf'), may hold values from 0 to 511
- leaf_coupling: float32 [16, 32, 131072], P(None, None, 'leaf'), may hold values from -0.25 to 0.25
- top_list: int32 [512, 8], P('leaf'), may hold values from 0 to 511
- top_coupling: float32 [8, 32, 16384], P(None, None, 'leaf'), may hold values from -0.375 to 0.375
Outputs:
- product: float32 [16, 262144], P('vec', 'leaf')
The draws below stay inside these ranges and needn't reach their ends.
Inputs may be any that keep to these rules, and one draw needn't show every extreme that they name: `near_list`: the 8 source leaves of a target leaf lie on the target's own device or on the devices just before and after it along leaf. The 8 entries of send_leaves[p, d] are distinct local leaves of device p. `send_counts`: every sender fills all 8 slots toward some receiver, and some receiver gets all 8 slots filled from every sender.
All inputs are finite; a program needn't handle non-finite values.
Results may differ from the reference program's by a relative error of at most 0.000058.
Values sent between devices are 32-bit elements; how exact they have to be, the bound alone decides.
No kernel may reach another device: no remote copies, remote signals or barrier semaphores. Data moves between devices by JAX's collectives and lax.ppermute only.
A program may use at most 128 MiB of HBM per device.

```python
import jax
import jax.numpy as jnp
from jax import lax

PTS = 64
RANK = 32
VECS = 16
LEAF_DEV = 64
FAR = 16
NEAR = 8
PFAR = 8
CAP = 8
LEAVES = 4096
POINTS = 262144
PARENTS = 512
N_LEAF = 64


def interaction_lists(key):
    subkeys = jax.random.split(key, 6)
    counts = jax.random.randint(subkeys[0], (N_LEAF, N_LEAF), 1, CAP + 1)
    column = jax.random.randint(subkeys[1], (), 0, N_LEAF)
    offset = jax.random.randint(subkeys[2], (), 1, N_LEAF)
    row_index = jnp.arange(N_LEAF)[:, None]
    col_index = jnp.arange(N_LEAF)[None, :]
    forced = (col_index == column) | (col_index == (row_index + offset) % N_LEAF)
    counts = jnp.where(forced, CAP, counts).astype(jnp.int32)
    scores = jax.random.randint(subkeys[3], (N_LEAF, N_LEAF, LEAF_DEV), 0, 2 ** 20) * LEAF_DEV + jnp.arange(LEAF_DEV)
    chosen = jnp.argsort(scores, axis=-1, stable=True)[:, :, :CAP].astype(jnp.int32)
    sender = jax.random.randint(subkeys[4], (LEAVES, FAR), 0, N_LEAF)
    slot_place = jax.random.randint(subkeys[5], (LEAVES, FAR), 0, CAP)
    slots = (sender * CAP + slot_place).astype(jnp.int32)
    slots = slots.at[0, 0].set(N_LEAF * CAP - 1).at[0, 1].set(0)
    return (counts, chosen, slots.astype(jnp.int32))


def draw_send_counts(key, part):
    return interaction_lists(key)[0]


def draw_send_leaves(key, part):
    return interaction_lists(key)[1]


def draw_recv_slot(key, part):
    return interaction_lists(key)[2]


def draw_near_list(key, part):
    key = jax.random.fold_in(key, 7)
    device_of = jnp.arange(LEAVES) // LEAF_DEV
    low_bound = jnp.maximum(device_of - 1, 0) * LEAF_DEV
    high_bound = jnp.minimum(device_of + 2, N_LEAF) * LEAF_DEV
    offsets = jax.random.randint(key, (LEAVES, NEAR), 0, 2 ** 20)
    listed = (low_bound[:, None] + offsets % (high_bound - low_bound)[:, None]).astype(jnp.int32)
    listed = listed.at[0, 0].set(0).at[LEAVES - 1, 0].set(LEAVES - 1)
    return listed.astype(jnp.int32)


def place_ends(entries, own_key, low, top_value):
    index_at = [jax.random.randint(jax.random.fold_in(own_key, axis), (), 0, length) for axis, length in enumerate(entries.shape)]
    longest = entries.shape.index(max(entries.shape))
    beside = index_at[:longest] + [(index_at[longest] + 1) % entries.shape[longest]] + index_at[longest + 1:]
    return entries.at[tuple(index_at)].set(low).at[tuple(beside)].set(top_value)


def block_scale(own_key, shape, cuts, least, high):
    gain = 1.0
    for dim, shards_of in cuts:
        heights = jax.random.uniform(jax.random.fold_in(jax.random.fold_in(own_key, 6), dim), (shards_of,), jnp.float32, least / len(cuts), high / len(cuts))
        gain = gain * jnp.repeat(jnp.exp(heights), shape[dim] // shards_of).reshape((-1,) + (1,) * (len(shape) - 1 - dim))
    return gain


def normal_values(own_key, shape, deviation, most, pieces=(), kind=jnp.bfloat16):
    result = deviation * jax.random.normal(own_key, shape, jnp.float32)
    if pieces:
        result = result * block_scale(own_key, shape, pieces, -0.22, 0.18)
    return jnp.clip(result, -most, most).astype(kind)


def setup_inputs(seed: int = 0) -> dict:
    keys = jax.random.split(jax.random.key(seed), 14)
    points_x = normal_values(keys[0], (VECS, POINTS), 1.0, 6.0, ((0, 4), (1, 64)), jnp.float32)
    near_list = draw_near_list(jax.random.fold_in(keys[13], 71), 0)
    near_blocks = normal_values(keys[2], (NEAR, PTS, POINTS), (PTS * NEAR) ** -0.5, 0.25, ((0, 4), (2, 64)), jnp.float32)
    leaf_basis = normal_values(keys[3], (RANK, POINTS), PTS ** -0.5, 0.75, ((1, 64),), jnp.float32)
    out_basis = normal_values(keys[4], (RANK, POINTS), RANK ** -0.5, 1.0, ((1, 64),), jnp.float32)
    up_transfer = normal_values(keys[5], (RANK, LEAVES * RANK), (8 * RANK) ** -0.5, 0.375, ((1, 64),), jnp.float32)
    down_transfer = normal_values(keys[6], (RANK, LEAVES * RANK), RANK ** -0.5, 1.0, ((1, 64),), jnp.float32)
    send_leaves = draw_send_leaves(jax.random.fold_in(keys[13], 71), 0)
    send_counts = draw_send_counts(jax.random.fold_in(keys[13], 71), 0)
    recv_slot = draw_recv_slot(jax.random.fold_in(keys[13], 71), 0)
    leaf_coupling = normal_values(keys[10], (FAR, RANK, LEAVES * RANK), (FAR * RANK) ** -0.5, 0.25, ((2, 64),), jnp.float32)
    top_list = place_ends(jax.random.randint(keys[11], (PARENTS, PFAR), 0, PARENTS), jax.random.fold_in(keys[11], 1), 0, PARENTS - 1).astype(jnp.int32)
    top_coupling = normal_values(keys[12], (PFAR, RANK, PARENTS * RANK), (PFAR * RANK) ** -0.5, 0.375, ((2, 64),), jnp.float32)
    return dict(points_x=points_x, near_list=near_list, near_blocks=near_blocks, leaf_basis=leaf_basis, out_basis=out_basis, up_transfer=up_transfer, down_transfer=down_transfer, send_leaves=send_leaves, send_counts=send_counts, recv_slot=recv_slot, leaf_coupling=leaf_coupling, top_list=top_list, top_coupling=top_coupling)


def contract(pattern, left, right):
    return jnp.einsum(pattern, left, right, precision=lax.Precision.HIGHEST)


def reference(points_x, near_list, near_blocks, leaf_basis, out_basis, up_transfer, down_transfer, send_leaves, send_counts, recv_slot, leaf_coupling, top_list, top_coupling):
    vectors = points_x.reshape(VECS, LEAVES, PTS)
    skeleton = contract('clp,rlp->lcr', vectors, leaf_basis.reshape(RANK, LEAVES, PTS))
    lifted = contract('lcr,rlq->lcq', skeleton, up_transfer.reshape(RANK, LEAVES, RANK))
    parents = lifted.reshape(PARENTS, 8, VECS, RANK).sum(axis=1)
    target_dev = (jnp.arange(LEAVES, dtype=jnp.int32) // LEAF_DEV)[:, None]
    sender = (recv_slot // CAP).astype(jnp.int32)
    slot_place = (recv_slot % CAP).astype(jnp.int32)
    source_leaf = send_leaves[sender, target_dev, slot_place] + sender * LEAF_DEV
    live_mask = (slot_place < send_counts[sender, target_dev]).astype(jnp.float32)
    gathered = skeleton[source_leaf] * live_mask[:, :, None, None]
    coupled = contract('ljcr,jrlq->lcq', gathered, leaf_coupling.reshape(FAR, RANK, LEAVES, RANK))
    top_tiles = parents[top_list]
    top_field = contract('qjcr,jrqs->qcs', top_tiles, top_coupling.reshape(PFAR, RANK, PARENTS, RANK))
    spread = jnp.repeat(top_field, 8, axis=0)
    down_part = contract('lcr,rlq->lcq', spread, down_transfer.reshape(RANK, LEAVES, RANK))
    local_field = coupled + down_part
    far_out = contract('lcr,rlp->clp', local_field, out_basis.reshape(RANK, LEAVES, PTS))
    near_source = vectors[:, near_list]
    near_out = contract('cljs,jslp->clp', near_source, near_blocks.reshape(NEAR, PTS, LEAVES, PTS))
    return (far_out + near_out).reshape(VECS, LEAVES * PTS)
```

```python
import jax
import jax.numpy as jnp
from jax import lax
from jax.experimental import pallas as pl
from jax.experimental.pallas import tpu as pltpu
from jax.sharding import PartitionSpec as P

PTS = 64
RANK = 32
GROUP = 8
LANES = 128
F32 = jnp.float32
BF16 = jnp.bfloat16


def iota(shape, dim):
    return lax.broadcasted_iota(jnp.int32, shape, dim)


def split(value):
    high = value.astype(BF16)
    return high, (value - high.astype(F32)).astype(BF16)


NN = (((1,), (0,)), ((), ()))
NT = (((1,), (1,)), ((), ()))


def mxu(left, right, dims=NN):
    return lax.dot_general(left, right, dims, preferred_element_type=F32)


def dot3(left, right, dims=NN):
    rows = left.shape[0]
    left_high, left_low = split(left)
    right_high, right_low = split(right)
    both = mxu(jnp.concatenate([left_high, left_low], axis=0), right_high, dims)
    return both[:rows] + both[rows:] + mxu(left_high, right_low, dims)


def fold(value):
    value = value[:, :LANES] + value[:, LANES:]
    value = value + pltpu.roll(value, 64, 1)
    return value + pltpu.roll(value, 32, 1)


def pick_rows(rows_of, table_high, table_low):
    count, columns = rows_of.shape
    entries = table_high.shape[0]
    lane = iota((count, entries), 1)
    hot = jnp.concatenate(
        [
            jnp.where(rows_of[:, j : j + 1] == lane, 1.0, 0.0).astype(BF16)
            for j in range(columns)
        ],
        axis=0,
    )
    got = mxu(hot, jnp.concatenate([table_high, table_low], axis=1))
    return got[:, :LANES] + got[:, LANES:]


def by_column(tiles, columns):
    block = iota((GROUP, LANES), 1) // RANK
    per = LANES // RANK
    rows = []
    for c in range(columns):
        pieces = []
        for first in range(0, len(tiles), per):
            piece = None
            for k in range(per):
                shift = ((k - c) * RANK) % LANES
                tile = tiles[first + k]
                moved = pltpu.roll(tile, shift, 1) if shift else tile
                piece = moved if piece is None else jnp.where(block == k, moved, piece)
            pieces.append(piece)
        rows.append(jnp.concatenate(pieces, axis=1))
    return jnp.concatenate(rows, axis=0)


def up_kernel(x_ref, basis_ref, up_ref, leaves_ref, counts_ref, send_ref):
    columns = x_ref.shape[0]
    leaf_count = x_ref.shape[1] // PTS
    peers, slots = leaves_ref.shape
    wide = GROUP * PTS
    own = iota((GROUP, wide), 1) // PTS == iota((GROUP, wide), 0)
    lane_block = iota((GROUP, LANES), 1) // RANK
    diagonal = iota((columns * GROUP, GROUP * RANK), 1) // RANK == (
        iota((columns * GROUP, GROUP * RANK), 0) % GROUP
    )
    skeleton, parents = [], []
    for q in range(leaf_count // GROUP):
        x = x_ref[:, q * wide : (q + 1) * wide]
        spread = jnp.concatenate(
            [jnp.where(own, x[c : c + 1], 0.0) for c in range(columns)], axis=0
        )
        tile = dot3(spread, basis_ref[:, q * wide : (q + 1) * wide], NT)
        skeleton.append(
            jnp.concatenate(
                [tile[c * GROUP : (c + 1) * GROUP] for c in range(columns)], axis=1
            )
        )
        narrow = GROUP * RANK
        lifted = dot3(tile, up_ref[:, q * narrow : (q + 1) * narrow])
        lifted = fold(jnp.where(diagonal, lifted, 0.0))
        total = None
        for c in range(columns):
            part = jnp.where(lane_block == c, lifted[c * GROUP : (c + 1) * GROUP], 0.0)
            total = part if total is None else total + part
        parents.append(jnp.sum(total, axis=0, keepdims=True))
    skeleton = jnp.concatenate(skeleton, axis=0)
    parents = jnp.concatenate(parents, axis=0)

    counts = jnp.broadcast_to(counts_ref[...].astype(F32), (peers, peers))
    square = iota((peers, peers), 0) == iota((peers, peers), 1)
    count_column = jnp.sum(jnp.where(square, counts, 0.0), axis=1, keepdims=True)
    wanted = jnp.where(
        iota((peers, slots), 1).astype(F32) < count_column, leaves_ref[...].astype(F32), -1.0
    )
    rows = peers * slots
    expand = jnp.where(iota((rows, peers), 0) // slots == iota((rows, peers), 1), 1.0, 0.0)
    wanted = mxu(expand.astype(BF16), wanted.astype(BF16))
    wanted = jnp.sum(
        jnp.where(iota((rows, slots), 0) % slots == iota((rows, slots), 1), wanted, 0.0),
        axis=1,
        keepdims=True,
    )
    hot = jnp.where(wanted == iota((rows, leaf_count), 1).astype(F32), 1.0, 0.0).astype(BF16)
    high, low = split(skeleton)
    got = mxu(hot, jnp.concatenate([high, low], axis=1))
    got = got[:, :LANES] + got[:, LANES:]
    send_ref[:, :slots, :] = got.reshape(peers, slots, LANES)
    par_count = parents.shape[0]
    send_ref[:, slots:, :] = jnp.broadcast_to(parents[None], (peers, par_count, LANES))


def near_kernel(list_ref, own_ref, left_ref, right_ref, blocks_ref, *rest):
    outs, table = rest[:-1], rest[-1]
    total_columns, points = own_ref.shape
    leaf_count = points // PTS
    share = blocks_ref.shape[0]
    columns = total_columns // len(outs)
    base = (lax.axis_index("leaf") - 1) * leaf_count
    first = lax.axis_index("vec") * share
    for place, ref in enumerate((left_ref, own_ref, right_ref)):
        for b in range(points // LANES):
            tile = ref[:, b * LANES : (b + 1) * LANES]
            at = place * (points // LANES) + b
            table[0, at] = tile
            table[1, at] = pltpu.roll(tile, PTS, 1)
    lower = iota((total_columns, LANES), 1) < PTS
    per = 4
    for g in range(leaf_count // per):
        tiles = []
        for i in range(per):
            t = g * per + i
            one = list_ref[t, first] - base
            two = list_ref[t, first + 1] - base
            tiles.append(
                jnp.where(
                    lower, table[one % 2, one // 2], table[1 - two % 2, two // 2]
                )
            )
        sources = jnp.concatenate(tiles, axis=0)
        lanes = slice(g * per * PTS, (g + 1) * per * PTS)
        block = blocks_ref[:, :, lanes].reshape(share * PTS, per * PTS)
        value = dot3(sources, block)
        for h in range(per // 2):
            at = 2 * h * total_columns
            cut = slice(h * LANES, (h + 1) * LANES)
            result = jnp.where(
                lower,
                value[at : at + total_columns, cut],
                value[at + total_columns : at + 2 * total_columns, cut],
            )
            place = slice((g * per // 2 + h) * LANES, (g * per // 2 + h + 1) * LANES)
            for s, out in enumerate(outs):
                out[:, place] = result[s * columns : (s + 1) * columns]


def far_kernel(
    recv_ref, slot_ref, top_ref, coupling_ref, top_coupling_ref, down_ref, basis_ref, out_ref
):
    columns, points = out_ref.shape
    leaf_count = points // PTS
    peers = recv_ref.shape[0]
    par_count = leaf_count // GROUP
    slots = recv_ref.shape[1] - par_count
    far_count = coupling_ref.shape[0]
    top_count = top_coupling_ref.shape[0]
    narrow, wide = GROUP * RANK, GROUP * PTS
    rows = columns * GROUP
    diagonal = iota((rows, narrow), 1) // RANK == iota((rows, narrow), 0) % GROUP
    diagonal_out = iota((rows, wide), 1) // PTS == iota((rows, wide), 0) % GROUP

    tops = recv_ref[:, slots:, :].reshape(peers * par_count, LANES)
    got = pick_rows(top_ref[...], *split(tops))
    field = dot3(
        by_column([got[j * GROUP : (j + 1) * GROUP] for j in range(top_count)], columns),
        top_coupling_ref[...].reshape(top_count * RANK, narrow),
    )
    field = fold(jnp.where(diagonal, field, 0.0))[:, :RANK]
    lowered = dot3(field, down_ref[...])

    tiles = recv_ref[:, :slots, :].reshape(peers * slots, LANES)
    got = pick_rows(slot_ref[...], *split(tiles))
    for g in range(par_count):
        sources = by_column(
            [
                got[j * leaf_count + g * GROUP : j * leaf_count + (g + 1) * GROUP]
                for j in range(far_count)
            ],
            columns,
        )
        lanes = slice(g * narrow, (g + 1) * narrow)
        value = dot3(sources, coupling_ref[:, :, lanes].reshape(far_count * RANK, narrow))
        value = value + jnp.concatenate(
            [
                jnp.broadcast_to(
                    lowered[c * GROUP + g : c * GROUP + g + 1, lanes], (GROUP, narrow)
                )
                for c in range(columns)
            ],
            axis=0,
        )
        local_field = fold(jnp.where(diagonal, value, 0.0))[:, :RANK]
        value = dot3(local_field, basis_ref[:, g * wide : (g + 1) * wide])
        value = jnp.where(diagonal_out, value, 0.0)
        out_ref[:, g * wide : (g + 1) * wide] = jnp.sum(
            value.reshape(columns, GROUP, wide), axis=1
        )


VMEM = pl.BlockSpec(memory_space=pltpu.VMEM)
SMEM = pl.BlockSpec(memory_space=pltpu.SMEM)
PARAMS = pltpu.CompilerParams(vmem_limit_bytes=40 * 1024 * 1024)


def local(
    points_x,
    near_list,
    near_blocks,
    leaf_basis,
    out_basis,
    up_transfer,
    down_transfer,
    send_leaves,
    send_counts,
    recv_slot,
    leaf_coupling,
    top_list,
    top_coupling,
):
    columns, points = points_x.shape
    leaf_count = near_list.shape[0]
    par_count = top_list.shape[0]
    peers, slots = send_leaves.shape[1:]
    groups = lax.axis_size("vec")
    ring = lax.axis_size("leaf")

    others = [
        lax.ppermute(points_x, "vec", [(i, (i + s) % groups) for i in range(groups)])
        for s in range(1, groups)
    ]
    send = pl.pallas_call(
        up_kernel,
        name="up",
        out_shape=jax.ShapeDtypeStruct((peers, slots + par_count, LANES), F32),
        in_specs=[VMEM] * 5,
        out_specs=VMEM,
        compiler_params=PARAMS,
    )(points_x, leaf_basis, up_transfer, send_leaves[0], send_counts)
    every = jnp.concatenate([points_x] + others, axis=0)
    left = lax.ppermute(every, "leaf", [(i, (i + 1) % ring) for i in range(ring)])
    right = lax.ppermute(every, "leaf", [((i + 1) % ring, i) for i in range(ring)])
    recv = lax.all_to_all(send, "leaf", split_axis=0, concat_axis=0, tiled=True)
    partial = pl.pallas_call(
        near_kernel,
        name="near",
        out_shape=[jax.ShapeDtypeStruct((columns, points), F32)] * groups,
        in_specs=[SMEM] + [VMEM] * 4,
        out_specs=[VMEM] * groups,
        scratch_shapes=[pltpu.VMEM((2, 3 * points // LANES, columns * groups, LANES), F32)],
        compiler_params=PARAMS,
        cost_estimate=pl.CostEstimate(
            flops=2 * near_blocks.size * columns * groups,
            bytes_accessed=4 * near_blocks.size,
            transcendentals=0,
        ),
    )(near_list, every, left, right, near_blocks)
    parts = [partial[0]] + [
        lax.ppermute(partial[s], "vec", [(i, (i - s) % groups) for i in range(groups)])
        for s in range(1, groups)
    ]
    far = pl.pallas_call(
        far_kernel,
        name="far",
        out_shape=jax.ShapeDtypeStruct((columns, points), F32),
        in_specs=[VMEM] * 7,
        out_specs=VMEM,
        compiler_params=PARAMS,
    )(recv, recv_slot, top_list, leaf_coupling, top_coupling, down_transfer, out_basis)
    return far + sum(parts[1:], parts[0])


def solution(mesh):
    placed = (
        P("vec", "leaf"),
        P("leaf", None),
        P("vec", None, "leaf"),
        P(None, "leaf"),
        P(None, "leaf"),
        P(None, "leaf"),
        P(None, "leaf"),
        P("leaf", None, None),
        P("leaf", None),
        P("leaf", None),
        P(None, None, "leaf"),
        P("leaf", None),
        P(None, None, "leaf"),
    )
    return jax.shard_map(
        local, mesh=mesh, in_specs=placed, out_specs=P("vec", "leaf"), check_vma=False
    )
```

```python
import jax
import jax.numpy as jnp
from jax import lax
from jax.experimental import pallas as pl
from jax.experimental.pallas import tpu as pltpu
from jax.sharding import PartitionSpec as P

PTS = 64
RANK = 32
GROUP = 8
LANES = 128
F32 = jnp.float32
BF16 = jnp.bfloat16


def iota(shape, dim):
    return lax.broadcasted_iota(jnp.int32, shape, dim)


def split(value):
    high = value.astype(BF16)
    return high, (value - high.astype(F32)).astype(BF16)


NN = (((1,), (0,)), ((), ()))
NT = (((1,), (1,)), ((), ()))


def mxu(left, right, dims=NN):
    return lax.dot_general(left, right, dims, preferred_element_type=F32)


def dot3(left, right, dims=NN):
    rows = left.shape[0]
    left_high, left_low = split(left)
    right_high, right_low = right if isinstance(right, tuple) else split(right)
    both = mxu(jnp.concatenate([left_high, left_low], axis=0), right_high, dims)
    return both[:rows] + both[rows:] + mxu(left_high, right_low, dims)


def fold(value):
    value = value[:, :LANES] + value[:, LANES:]
    value = value + pltpu.roll(value, 64, 1)
    return value + pltpu.roll(value, 32, 1)


def hot_rows(rows_of, entries):
    count, columns = rows_of.shape
    lane = iota((count, entries), 1)
    return jnp.concatenate(
        [
            jnp.where(rows_of[:, j : j + 1] == lane, 1.0, 0.0).astype(BF16)
            for j in range(columns)
        ],
        axis=0,
    )


def pick_rows(hot, table):
    got = mxu(hot, jnp.concatenate(split(table), axis=1))
    return got[:, :LANES] + got[:, LANES:]


def by_column(tiles, columns):
    block = iota((GROUP, LANES), 1) // RANK
    per = LANES // RANK
    rows = []
    for c in range(columns):
        pieces = []
        for first in range(0, len(tiles), per):
            piece = None
            for k in range(per):
                shift = ((k - c) * RANK) % LANES
                tile = tiles[first + k]
                moved = pltpu.roll(tile, shift, 1) if shift else tile
                piece = moved if piece is None else jnp.where(block == k, moved, piece)
            pieces.append(piece)
        rows.append(jnp.concatenate(pieces, axis=1))
    return jnp.concatenate(rows, axis=0)


def fetch(sources, targets, sems):
    copies = [
        pltpu.make_async_copy(source, target, sems.at[i])
        for i, (source, target) in enumerate(zip(sources, targets))
    ]
    for copy in copies:
        copy.start()
    return copies


def up_kernel(x_in, basis_in, up_in, leaves_in, counts_in, send_ref, *scratch):
    x_ref, basis_ref, up_ref, leaves_ref, counts_ref, sems = scratch
    for copy in fetch((x_in, basis_in, up_in, leaves_in, counts_in), scratch[:5], sems):
        copy.wait()
    columns = x_ref.shape[0]
    leaf_count = x_ref.shape[1] // PTS
    slots, peers = leaves_ref.shape
    wide = GROUP * PTS
    own = iota((GROUP, wide), 1) // PTS == iota((GROUP, wide), 0)
    lane_block = iota((GROUP, LANES), 1) // RANK
    diagonal = iota((columns * GROUP, GROUP * RANK), 1) // RANK == (
        iota((columns * GROUP, GROUP * RANK), 0) % GROUP
    )
    narrow = GROUP * RANK
    tiles = []
    for q in range(leaf_count // GROUP):
        x = x_ref[:, q * wide : (q + 1) * wide]
        spread = jnp.concatenate(
            [jnp.where(own, x[c : c + 1], 0.0) for c in range(columns)], axis=0
        )
        tiles.append(dot3(spread, basis_ref[:, q * wide : (q + 1) * wide], NT))
    lifted = [
        dot3(tile, up_ref[:, q * narrow : (q + 1) * narrow]) for q, tile in enumerate(tiles)
    ]
    skeleton = jnp.concatenate(
        [
            jnp.concatenate(
                [tile[c * GROUP : (c + 1) * GROUP] for c in range(columns)], axis=1
            )
            for tile in tiles
        ],
        axis=0,
    )
    parents = []
    for value in lifted:
        value = fold(jnp.where(diagonal, value, 0.0))
        total = None
        for c in range(columns):
            part = jnp.where(lane_block == c, value[c * GROUP : (c + 1) * GROUP], 0.0)
            total = part if total is None else total + part
        parents.append(jnp.sum(total, axis=0, keepdims=True))
    parents = jnp.concatenate(parents, axis=0)

    wanted = jnp.where(
        iota((slots, peers), 0) < counts_ref[...], leaves_ref[...].astype(F32), -1.0
    )
    rows = peers * slots
    expand = jnp.where(iota((rows, peers), 0) // slots == iota((rows, peers), 1), 1.0, 0.0)
    wanted = mxu(expand.astype(BF16), wanted.astype(BF16), NT)
    wanted = jnp.sum(
        jnp.where(iota((rows, slots), 0) % slots == iota((rows, slots), 1), wanted, 0.0),
        axis=1,
        keepdims=True,
    )
    hot = jnp.where(wanted == iota((rows, leaf_count), 1).astype(F32), 1.0, 0.0).astype(BF16)
    high, low = split(skeleton)
    got = mxu(hot, jnp.concatenate([high, low], axis=1))
    got = got[:, :LANES] + got[:, LANES:]
    send_ref[:, :slots, :] = got.reshape(peers, slots, LANES)
    par_count = parents.shape[0]
    send_ref[:, slots:, :] = jnp.broadcast_to(parents[None], (peers, par_count, LANES))


def pick_kernel(list_in, own_ref, left_ref, right_ref, *rest):
    outs, (table, list_ref, sems) = rest[:-3], rest[-3:]
    copies = fetch((list_in,), (list_ref,), sems)
    columns, points = own_ref.shape
    leaf_count = points // PTS
    groups = len(outs)
    share = list_ref.shape[0] // groups
    base = (lax.axis_index("leaf") - 1) * leaf_count
    me = lax.axis_index("vec")
    for place, ref in enumerate((left_ref, own_ref, right_ref)):
        for b in range(points // LANES):
            tile = ref[:, b * LANES : (b + 1) * LANES]
            tile = jnp.concatenate([tile, tile], axis=0)
            at = place * (points // LANES) + b
            table[0, at] = tile
            table[1, at] = pltpu.roll(tile, PTS, 1)
    lower = iota((2 * columns, LANES), 1) < PTS
    upper_rows = iota((2 * columns, LANES), 0) >= columns
    for copy in copies:
        copy.wait()
    for s, out in enumerate(outs):
        first = lax.rem(me + s, groups) * share
        for pair in range(leaf_count // 2):
            halves = []
            for t in (2 * pair, 2 * pair + 1):
                one = list_ref[first, t] - base
                two = list_ref[first + 1, t] - base
                halves.append(
                    jnp.where(lower, table[one & 1, one >> 1], table[1 - (two & 1), two >> 1])
                )
            out[pair] = jnp.where(upper_rows, halves[1], halves[0])


def near_kernel(blocks_in, *rest):
    blocks_ref, sems = rest[-2:]
    copies = fetch((blocks_in,), (blocks_ref,), sems)
    groups = (len(rest) - 2) // 2
    parts, outs = rest[:groups], rest[groups : 2 * groups]
    columns, points = outs[0].shape
    share = blocks_ref.shape[0]
    lower = iota((columns, LANES), 1) < PTS
    rows = 2 * columns
    per = 2
    for copy in copies:
        copy.wait()
    for g in range(points // (per * LANES)):
        sources = jnp.concatenate(
            [part[g * per + h] for h in range(per) for part in parts], axis=0
        )
        block = blocks_ref[:, :, g * per * LANES : (g + 1) * per * LANES]
        value = dot3(sources, block.reshape(share * PTS, per * LANES))
        for h in range(per):
            for s, out in enumerate(outs):
                at = (h * groups + s) * rows
                tile = value[at : at + rows, h * LANES : (h + 1) * LANES]
                out[:, (g * per + h) * LANES : (g * per + h + 1) * LANES] = jnp.where(
                    lower, tile[:columns], tile[columns:]
                )


def far_kernel(*refs):
    count = 7
    sources, out_ref, targets, (hot_ref, sems) = refs[:7], refs[7], refs[8:15], refs[15:]
    recv_ref, top_ref, slot_ref, top_coupling_ref, down_ref, coupling_ref, basis_ref = targets
    coupling_in = sources[5]
    columns, points = out_ref.shape
    leaf_count = points // PTS
    peers = recv_ref.shape[0]
    par_count = leaf_count // GROUP
    slots = recv_ref.shape[1] - par_count
    far_count = coupling_ref.shape[0]
    top_count = top_coupling_ref.shape[0]
    narrow, wide = GROUP * RANK, GROUP * PTS
    groups = range(par_count)

    def lanes(g, size):
        return slice(g * size, (g + 1) * size)

    copies = []
    for i in range(count):
        if i != 5:
            copies.append(pltpu.make_async_copy(sources[i], targets[i], sems.at[i]))
    copies[5:5] = [
        pltpu.make_async_copy(
            coupling_in.at[:, :, lanes(g, narrow)],
            coupling_ref.at[:, :, lanes(g, narrow)],
            sems.at[count + g],
        )
        for g in groups
    ]
    for copy in copies:
        copy.start()
    rows = columns * GROUP
    diagonal = iota((rows, narrow), 1) // RANK == iota((rows, narrow), 0) % GROUP
    diagonal_out = iota((rows, wide), 1) // PTS == iota((rows, wide), 0) % GROUP

    copies[1].wait()
    copies[2].wait()
    square = iota((leaf_count, leaf_count), 0) == iota((leaf_count, leaf_count), 1)
    square = jnp.where(square, 1.0, 0.0).astype(BF16)
    slot = slot_ref[...]
    slot = mxu(square, (slot >> 5).astype(F32).astype(BF16), NT) * 32.0 + mxu(
        square, (slot & 31).astype(F32).astype(BF16), NT
    )
    hot_top = hot_rows(top_ref[...], peers * par_count)
    hot_ref[...] = hot_rows(slot.astype(jnp.int32), peers * slots)
    copies[0].wait()
    tops = recv_ref[:, slots:, :].reshape(peers * par_count, LANES)
    top_got = pick_rows(hot_top, tops)
    tiles = recv_ref[:, :slots, :].reshape(peers * slots, LANES)
    got = pick_rows(hot_ref[...], tiles)

    for copy in copies[3:5]:
        copy.wait()
    field = dot3(
        by_column([top_got[lanes(j, GROUP)] for j in range(top_count)], columns),
        top_coupling_ref[...].reshape(top_count * RANK, narrow),
    )
    field = fold(jnp.where(diagonal, field, 0.0))[:, :RANK]
    lowered = dot3(field, down_ref[...])

    gathered = [
        by_column(
            [got[lanes(j * par_count + g, GROUP)] for j in range(far_count)],
            columns,
        )
        for g in groups
    ]
    fields = []
    for g in groups:
        copies[5 + g].wait()
        fields.append(
            dot3(
                gathered[g],
                coupling_ref[:, :, lanes(g, narrow)].reshape(far_count * RANK, narrow),
            )
        )
    spread = []
    for g in groups:
        above = jnp.concatenate(
            [
                jnp.broadcast_to(
                    lowered[c * GROUP + g : c * GROUP + g + 1, lanes(g, narrow)], (GROUP, narrow)
                )
                for c in range(columns)
            ],
            axis=0,
        )
        spread.append(fold(jnp.where(diagonal, fields[g] + above, 0.0))[:, :RANK])
    for copy in copies[5 + par_count :]:
        copy.wait()
    values = [dot3(spread[g], basis_ref[:, lanes(g, wide)]) for g in groups]
    for g in groups:
        value = jnp.where(diagonal_out, values[g], 0.0)
        out_ref[:, lanes(g, wide)] = jnp.sum(value.reshape(columns, GROUP, wide), axis=1)


VMEM = pl.BlockSpec(memory_space=pltpu.VMEM)
ANY = pl.BlockSpec(memory_space=pl.ANY)
MIB = 1024 * 1024
UP_MIB, PICK_MIB, NEAR_MIB, FAR_MIB = 60, 24, 24, 60
UP_US, PICK_US, NEAR_US, FAR_US = 2, 2, 8, 4


def cost(micros):
    return pl.CostEstimate(flops=int(micros * 1e9), bytes_accessed=0, transcendentals=0)


def buffers(*arrays):
    return [pltpu.VMEM(array.shape, array.dtype) for array in arrays] + [
        pltpu.SemaphoreType.DMA((len(arrays),))
    ]


def local(
    points_x,
    near_list,
    near_blocks,
    leaf_basis,
    out_basis,
    up_transfer,
    down_transfer,
    send_leaves,
    send_counts,
    recv_slot,
    leaf_coupling,
    top_list,
    top_coupling,
):
    columns, points = points_x.shape
    leaf_count = near_list.shape[0]
    par_count = top_list.shape[0]
    peers, slots = send_leaves.shape[1:]
    groups = lax.axis_size("vec")
    ring = lax.axis_size("leaf")

    left = lax.ppermute(points_x, "leaf", [(i, (i + 1) % ring) for i in range(ring)])
    right = lax.ppermute(points_x, "leaf", [((i + 1) % ring, i) for i in range(ring)])

    up_args = (points_x, leaf_basis, up_transfer, send_leaves[0].T, send_counts)
    send = pl.pallas_call(
        up_kernel,
        name="up",
        out_shape=jax.ShapeDtypeStruct((peers, slots + par_count, LANES), F32),
        in_specs=[ANY] * 5,
        out_specs=VMEM,
        scratch_shapes=buffers(*up_args),
        compiler_params=pltpu.CompilerParams(vmem_limit_bytes=UP_MIB * MIB),
        cost_estimate=cost(UP_US),
    )(*up_args)
    recv = lax.all_to_all(send, "leaf", split_axis=0, concat_axis=0, tiled=True)

    picked = pl.pallas_call(
        pick_kernel,
        name="pick",
        out_shape=[jax.ShapeDtypeStruct((leaf_count // 2, 2 * columns, LANES), F32)] * groups,
        in_specs=[ANY] + [VMEM] * 3,
        out_specs=[VMEM] * groups,
        scratch_shapes=[
            pltpu.VMEM((2, 3 * points // LANES, 2 * columns, LANES), F32),
            pltpu.SMEM(near_list.T.shape, jnp.int32),
            pltpu.SemaphoreType.DMA((1,)),
        ],
        compiler_params=pltpu.CompilerParams(vmem_limit_bytes=PICK_MIB * MIB),
        cost_estimate=cost(PICK_US),
    )(near_list.T, points_x, left, right)
    parts = [picked[0]] + [
        lax.ppermute(picked[s], "vec", [(i, (i + s) % groups) for i in range(groups)])
        for s in range(1, groups)
    ]

    partial = pl.pallas_call(
        near_kernel,
        name="near",
        out_shape=[jax.ShapeDtypeStruct((columns, points), F32)] * groups,
        in_specs=[ANY] + [VMEM] * groups,
        out_specs=[VMEM] * groups,
        scratch_shapes=buffers(near_blocks),
        compiler_params=pltpu.CompilerParams(vmem_limit_bytes=NEAR_MIB * MIB),
        cost_estimate=cost(NEAR_US),
    )(near_blocks, *parts)
    sums = [partial[0]] + [
        lax.ppermute(partial[s], "vec", [(i, (i - s) % groups) for i in range(groups)])
        for s in range(1, groups)
    ]
    far_args = [
        recv,
        top_list,
        recv_slot.T,
        top_coupling,
        down_transfer,
        leaf_coupling,
        out_basis,
    ]
    far = pl.pallas_call(
        far_kernel,
        name="far",
        out_shape=jax.ShapeDtypeStruct((columns, points), F32),
        in_specs=[ANY] * len(far_args),
        out_specs=VMEM,
        scratch_shapes=[pltpu.VMEM(array.shape, array.dtype) for array in far_args]
        + [
            pltpu.VMEM((recv_slot.size, peers * slots), BF16),
            pltpu.SemaphoreType.DMA((len(far_args) + par_count,)),
        ],
        compiler_params=pltpu.CompilerParams(vmem_limit_bytes=FAR_MIB * MIB),
        cost_estimate=cost(FAR_US),
    )(*far_args)
    return far + sum(sums[1:], sums[0])


def solution(mesh):
    placed = (
        P("vec", "leaf"),
        P("leaf", None),
        P("vec", None, "leaf"),
        P(None, "leaf"),
        P(None, "leaf"),
        P(None, "leaf"),
        P(None, "leaf"),
        P("leaf", None, None),
        P("leaf", None),
        P("leaf", None),
        P(None, None, "leaf"),
        P("leaf", None),
        P(None, None, "leaf"),
    )
    return jax.shard_map(
        local, mesh=mesh, in_specs=placed, out_specs=P("vec", "leaf"), check_vma=False
    )
```

```python
import jax
import jax.numpy as jnp
from jax import lax
from jax.experimental import pallas as pl
from jax.experimental.pallas import tpu as pltpu
from jax.sharding import PartitionSpec as P

PTS = 64
RANK = 32
GROUP = 8
LANES = 128
F32 = jnp.float32
BF16 = jnp.bfloat16


def iota(shape, dim):
    return lax.broadcasted_iota(jnp.int32, shape, dim)


def split(value):
    high = value.astype(BF16)
    return high, (value - high.astype(F32)).astype(BF16)


NN = (((1,), (0,)), ((), ()))
NT = (((1,), (1,)), ((), ()))


def mxu(left, right, dims=NN):
    return lax.dot_general(left, right, dims, preferred_element_type=F32)


def dot3(left, right, dims=NN):
    rows = left.shape[0]
    left_high, left_low = split(left)
    right_high, right_low = right if isinstance(right, tuple) else split(right)
    both = mxu(jnp.concatenate([left_high, left_low], axis=0), right_high, dims)
    return both[:rows] + both[rows:] + mxu(left_high, right_low, dims)


def fold(value):
    value = value[:, :LANES] + value[:, LANES:]
    value = value + pltpu.roll(value, 64, 1)
    return value + pltpu.roll(value, 32, 1)


def hot_rows(rows_of, entries):
    count, columns = rows_of.shape
    lane = iota((count, entries), 1)
    return jnp.concatenate(
        [
            jnp.where(rows_of[:, j : j + 1] == lane, 1.0, 0.0).astype(BF16)
            for j in range(columns)
        ],
        axis=0,
    )


def pick_rows(hot, table):
    got = mxu(hot, jnp.concatenate(split(table), axis=1))
    return got[:, :LANES] + got[:, LANES:]


def by_column(tiles, columns):
    block = iota((GROUP, LANES), 1) // RANK
    per = LANES // RANK
    rows = []
    for c in range(columns):
        pieces = []
        for first in range(0, len(tiles), per):
            piece = None
            for k in range(per):
                shift = ((k - c) * RANK) % LANES
                tile = tiles[first + k]
                moved = pltpu.roll(tile, shift, 1) if shift else tile
                piece = moved if piece is None else jnp.where(block == k, moved, piece)
            pieces.append(piece)
        rows.append(jnp.concatenate(pieces, axis=1))
    return jnp.concatenate(rows, axis=0)


def fetch(sources, targets, sems):
    copies = [
        pltpu.make_async_copy(source, target, sems.at[i])
        for i, (source, target) in enumerate(zip(sources, targets))
    ]
    for copy in copies:
        copy.start()
    return copies


def up_kernel(x_in, basis_in, up_in, leaves_in, counts_in, send_ref, *scratch):
    x_ref, basis_ref, up_ref, leaves_ref, counts_ref, sems = scratch
    for copy in fetch((x_in, basis_in, up_in, leaves_in, counts_in), scratch[:5], sems):
        copy.wait()
    columns = x_ref.shape[0]
    leaf_count = x_ref.shape[1] // PTS
    slots, peers = leaves_ref.shape
    wide = GROUP * PTS
    own = iota((GROUP, wide), 1) // PTS == iota((GROUP, wide), 0)
    lane_block = iota((GROUP, LANES), 1) // RANK
    diagonal = iota((columns * GROUP, GROUP * RANK), 1) // RANK == (
        iota((columns * GROUP, GROUP * RANK), 0) % GROUP
    )
    narrow = GROUP * RANK
    tiles = []
    for q in range(leaf_count // GROUP):
        x = x_ref[:, q * wide : (q + 1) * wide]
        spread = jnp.concatenate(
            [jnp.where(own, x[c : c + 1], 0.0) for c in range(columns)], axis=0
        )
        tiles.append(dot3(spread, basis_ref[:, q * wide : (q + 1) * wide], NT))
    lifted = [
        dot3(tile, up_ref[:, q * narrow : (q + 1) * narrow]) for q, tile in enumerate(tiles)
    ]
    skeleton = jnp.concatenate(
        [
            jnp.concatenate(
                [tile[c * GROUP : (c + 1) * GROUP] for c in range(columns)], axis=1
            )
            for tile in tiles
        ],
        axis=0,
    )
    parents = []
    for value in lifted:
        value = fold(jnp.where(diagonal, value, 0.0))
        total = None
        for c in range(columns):
            part = jnp.where(lane_block == c, value[c * GROUP : (c + 1) * GROUP], 0.0)
            total = part if total is None else total + part
        parents.append(jnp.sum(total, axis=0, keepdims=True))
    parents = jnp.concatenate(parents, axis=0)

    wanted = jnp.where(
        iota((slots, peers), 0) < counts_ref[...], leaves_ref[...].astype(F32), -1.0
    )
    rows = peers * slots
    expand = jnp.where(iota((rows, peers), 0) // slots == iota((rows, peers), 1), 1.0, 0.0)
    wanted = mxu(expand.astype(BF16), wanted.astype(BF16), NT)
    wanted = jnp.sum(
        jnp.where(iota((rows, slots), 0) % slots == iota((rows, slots), 1), wanted, 0.0),
        axis=1,
        keepdims=True,
    )
    hot = jnp.where(wanted == iota((rows, leaf_count), 1).astype(F32), 1.0, 0.0).astype(BF16)
    high, low = split(skeleton)
    got = mxu(hot, jnp.concatenate([high, low], axis=1))
    got = got[:, :LANES] + got[:, LANES:]
    send_ref[:, :slots, :] = got.reshape(peers, slots, LANES)
    par_count = parents.shape[0]
    send_ref[:, slots:, :] = jnp.broadcast_to(parents[None], (peers, par_count, LANES))


def pick_kernel(list_in, own_ref, left_ref, right_ref, *rest):
    outs, (table, list_ref, sems) = rest[:-3], rest[-3:]
    copies = fetch((list_in,), (list_ref,), sems)
    columns, points = own_ref.shape
    leaf_count = points // PTS
    groups = len(outs)
    share = list_ref.shape[0] // groups
    base = (lax.axis_index("leaf") - 1) * leaf_count
    me = lax.axis_index("vec")
    for place, ref in enumerate((left_ref, own_ref, right_ref)):
        for b in range(points // LANES):
            tile = ref[:, b * LANES : (b + 1) * LANES]
            tile = jnp.concatenate([tile, tile], axis=0)
            at = place * (points // LANES) + b
            table[0, at] = tile
            table[1, at] = pltpu.roll(tile, PTS, 1)
    lower = iota((2 * columns, LANES), 1) < PTS
    upper_rows = iota((2 * columns, LANES), 0) >= columns
    for copy in copies:
        copy.wait()
    for s, out in enumerate(outs):
        first = lax.rem(me + s, groups) * share
        for pair in range(leaf_count // 2):
            halves = []
            for t in (2 * pair, 2 * pair + 1):
                one = list_ref[first, t] - base
                two = list_ref[first + 1, t] - base
                halves.append(
                    jnp.where(lower, table[one & 1, one >> 1], table[1 - (two & 1), two >> 1])
                )
            out[pair] = jnp.where(upper_rows, halves[1], halves[0])


def near_kernel(blocks_in, *rest):
    blocks_ref, sems = rest[-2:]
    copies = fetch((blocks_in,), (blocks_ref,), sems)
    groups = (len(rest) - 2) // 2
    parts, outs = rest[:groups], rest[groups : 2 * groups]
    columns, points = outs[0].shape
    share = blocks_ref.shape[0]
    lower = iota((columns, LANES), 1) < PTS
    rows = 2 * columns
    per = 2
    for copy in copies:
        copy.wait()
    for g in range(points // (per * LANES)):
        sources = jnp.concatenate(
            [part[g * per + h] for h in range(per) for part in parts], axis=0
        )
        block = blocks_ref[:, :, g * per * LANES : (g + 1) * per * LANES]
        value = dot3(sources, block.reshape(share * PTS, per * LANES))
        for h in range(per):
            for s, out in enumerate(outs):
                at = (h * groups + s) * rows
                tile = value[at : at + rows, h * LANES : (h + 1) * LANES]
                out[:, (g * per + h) * LANES : (g * per + h + 1) * LANES] = jnp.where(
                    lower, tile[:columns], tile[columns:]
                )


def far_kernel(*refs):
    recv_ref, sources, out_ref, targets, (hot_ref, sems) = (
        refs[0],
        refs[1:7],
        refs[7],
        refs[8:14],
        refs[14:],
    )
    top_ref, slot_ref, top_coupling_ref, down_ref, coupling_ref, basis_ref = targets
    coupling_in = sources[4]
    columns, points = out_ref.shape
    leaf_count = points // PTS
    peers = recv_ref.shape[0]
    par_count = leaf_count // GROUP
    slots = recv_ref.shape[1] - par_count
    far_count = coupling_ref.shape[0]
    top_count = top_coupling_ref.shape[0]
    narrow, wide = GROUP * RANK, GROUP * PTS
    groups = range(par_count)

    def lanes(g, size):
        return slice(g * size, (g + 1) * size)

    copies = [
        pltpu.make_async_copy(sources[i], targets[i], sems.at[i]) for i in (0, 1, 2, 3, 5)
    ]
    copies[4:4] = [
        pltpu.make_async_copy(
            coupling_in.at[:, :, lanes(g, narrow)],
            coupling_ref.at[:, :, lanes(g, narrow)],
            sems.at[6 + g],
        )
        for g in groups
    ]
    for copy in copies:
        copy.start()
    rows = columns * GROUP
    diagonal = iota((rows, narrow), 1) // RANK == iota((rows, narrow), 0) % GROUP
    diagonal_out = iota((rows, wide), 1) // PTS == iota((rows, wide), 0) % GROUP

    copies[0].wait()
    copies[1].wait()
    square = iota((leaf_count, leaf_count), 0) == iota((leaf_count, leaf_count), 1)
    square = jnp.where(square, 1.0, 0.0).astype(BF16)
    slot = slot_ref[...]
    slot = mxu(square, (slot >> 5).astype(F32).astype(BF16), NT) * 32.0 + mxu(
        square, (slot & 31).astype(F32).astype(BF16), NT
    )
    hot_top = hot_rows(top_ref[...], peers * par_count)
    hot_ref[...] = hot_rows(slot.astype(jnp.int32), peers * slots)
    tops = recv_ref[:, slots:, :].reshape(peers * par_count, LANES)
    top_got = pick_rows(hot_top, tops)
    tiles = recv_ref[:, :slots, :].reshape(peers * slots, LANES)
    got = pick_rows(hot_ref[...], tiles)

    for copy in copies[2:4]:
        copy.wait()
    field = dot3(
        by_column([top_got[lanes(j, GROUP)] for j in range(top_count)], columns),
        top_coupling_ref[...].reshape(top_count * RANK, narrow),
    )
    field = fold(jnp.where(diagonal, field, 0.0))[:, :RANK]
    lowered = dot3(field, down_ref[...])

    gathered = [
        by_column(
            [got[lanes(j * par_count + g, GROUP)] for j in range(far_count)],
            columns,
        )
        for g in groups
    ]
    fields = []
    for g in groups:
        copies[4 + g].wait()
        fields.append(
            dot3(
                gathered[g],
                coupling_ref[:, :, lanes(g, narrow)].reshape(far_count * RANK, narrow),
            )
        )
    spread = []
    for g in groups:
        above = jnp.concatenate(
            [
                jnp.broadcast_to(
                    lowered[c * GROUP + g : c * GROUP + g + 1, lanes(g, narrow)], (GROUP, narrow)
                )
                for c in range(columns)
            ],
            axis=0,
        )
        spread.append(fold(jnp.where(diagonal, fields[g] + above, 0.0))[:, :RANK])
    for copy in copies[4 + par_count :]:
        copy.wait()
    values = [dot3(spread[g], basis_ref[:, lanes(g, wide)]) for g in groups]
    for g in groups:
        value = jnp.where(diagonal_out, values[g], 0.0)
        out_ref[:, lanes(g, wide)] = jnp.sum(value.reshape(columns, GROUP, wide), axis=1)


VMEM = pl.BlockSpec(memory_space=pltpu.VMEM)
ANY = pl.BlockSpec(memory_space=pl.ANY)
MIB = 1024 * 1024
UP_MIB, PICK_MIB, NEAR_MIB, FAR_MIB = 60, 24, 24, 51
UP_US, PICK_US, NEAR_US, FAR_US = 2, 2, 8, 4


def cost(micros):
    return pl.CostEstimate(flops=int(micros * 1e9), bytes_accessed=0, transcendentals=0)


def buffers(*arrays):
    return [pltpu.VMEM(array.shape, array.dtype) for array in arrays] + [
        pltpu.SemaphoreType.DMA((len(arrays),))
    ]


def local(
    points_x,
    near_list,
    near_blocks,
    leaf_basis,
    out_basis,
    up_transfer,
    down_transfer,
    send_leaves,
    send_counts,
    recv_slot,
    leaf_coupling,
    top_list,
    top_coupling,
):
    columns, points = points_x.shape
    leaf_count = near_list.shape[0]
    par_count = top_list.shape[0]
    peers, slots = send_leaves.shape[1:]
    groups = lax.axis_size("vec")
    ring = lax.axis_size("leaf")

    left = lax.ppermute(points_x, "leaf", [(i, (i + 1) % ring) for i in range(ring)])
    right = lax.ppermute(points_x, "leaf", [((i + 1) % ring, i) for i in range(ring)])

    up_args = (points_x, leaf_basis, up_transfer, send_leaves[0].T, send_counts)
    send = pl.pallas_call(
        up_kernel,
        name="up",
        out_shape=jax.ShapeDtypeStruct((peers, slots + par_count, LANES), F32),
        in_specs=[ANY] * 5,
        out_specs=VMEM,
        scratch_shapes=buffers(*up_args),
        compiler_params=pltpu.CompilerParams(vmem_limit_bytes=UP_MIB * MIB),
        cost_estimate=cost(UP_US),
    )(*up_args)
    recv = lax.all_to_all(send, "leaf", split_axis=0, concat_axis=0, tiled=True)

    picked = pl.pallas_call(
        pick_kernel,
        name="pick",
        out_shape=[jax.ShapeDtypeStruct((leaf_count // 2, 2 * columns, LANES), F32)] * groups,
        in_specs=[ANY] + [VMEM] * 3,
        out_specs=[VMEM] * groups,
        scratch_shapes=[
            pltpu.VMEM((2, 3 * points // LANES, 2 * columns, LANES), F32),
            pltpu.SMEM(near_list.T.shape, jnp.int32),
            pltpu.SemaphoreType.DMA((1,)),
        ],
        compiler_params=pltpu.CompilerParams(vmem_limit_bytes=PICK_MIB * MIB),
        cost_estimate=cost(PICK_US),
    )(near_list.T, points_x, left, right)
    parts = [picked[0]] + [
        lax.ppermute(picked[s], "vec", [(i, (i + s) % groups) for i in range(groups)])
        for s in range(1, groups)
    ]

    partial = pl.pallas_call(
        near_kernel,
        name="near",
        out_shape=[jax.ShapeDtypeStruct((columns, points), F32)] * groups,
        in_specs=[ANY] + [VMEM] * groups,
        out_specs=[VMEM] * groups,
        scratch_shapes=buffers(near_blocks),
        compiler_params=pltpu.CompilerParams(vmem_limit_bytes=NEAR_MIB * MIB),
        cost_estimate=cost(NEAR_US),
    )(near_blocks, *parts)
    sums = [partial[0]] + [
        lax.ppermute(partial[s], "vec", [(i, (i - s) % groups) for i in range(groups)])
        for s in range(1, groups)
    ]
    far_args = [
        top_list,
        recv_slot.T,
        top_coupling,
        down_transfer,
        leaf_coupling,
        out_basis,
    ]
    far = pl.pallas_call(
        far_kernel,
        name="far",
        out_shape=jax.ShapeDtypeStruct((columns, points), F32),
        in_specs=[VMEM] + [ANY] * len(far_args),
        out_specs=VMEM,
        scratch_shapes=[pltpu.VMEM(array.shape, array.dtype) for array in far_args]
        + [
            pltpu.VMEM((recv_slot.size, peers * slots), BF16),
            pltpu.SemaphoreType.DMA((len(far_args) + par_count,)),
        ],
        compiler_params=pltpu.CompilerParams(vmem_limit_bytes=FAR_MIB * MIB),
        cost_estimate=cost(FAR_US),
    )(recv, *far_args)
    return far + sum(sums[1:], sums[0])


def solution(mesh):
    placed = (
        P("vec", "leaf"),
        P("leaf", None),
        P("vec", None, "leaf"),
        P(None, "leaf"),
        P(None, "leaf"),
        P(None, "leaf"),
        P(None, "leaf"),
        P("leaf", None, None),
        P("leaf", None),
        P("leaf", None),
        P(None, None, "leaf"),
        P("leaf", None),
        P(None, None, "leaf"),
    )
    return jax.shard_map(
        local, mesh=mesh, in_specs=placed, out_specs=P("vec", "leaf"), check_vma=False
    )
```

```python
import jax
import jax.numpy as jnp
from jax import lax
from jax.experimental import pallas as pl
from jax.experimental.pallas import tpu as pltpu
from jax.sharding import PartitionSpec as P

PTS = 64
RANK = 32
GROUP = 8
LANES = 128
F32 = jnp.float32
BF16 = jnp.bfloat16


def iota(shape, dim):
    return lax.broadcasted_iota(jnp.int32, shape, dim)


def split(value):
    high = value.astype(BF16)
    return high, (value - high.astype(F32)).astype(BF16)


NN = (((1,), (0,)), ((), ()))
NT = (((1,), (1,)), ((), ()))


def mxu(left, right, dims=NN):
    return lax.dot_general(left, right, dims, preferred_element_type=F32)


def dot3(left, right, dims=NN):
    rows = left.shape[0]
    left_high, left_low = split(left)
    right_high, right_low = right if isinstance(right, tuple) else split(right)
    both = mxu(jnp.concatenate([left_high, left_low], axis=0), right_high, dims)
    return both[:rows] + both[rows:] + mxu(left_high, right_low, dims)


def fold(value):
    value = value[:, :LANES] + value[:, LANES:]
    value = value + pltpu.roll(value, 64, 1)
    return value + pltpu.roll(value, 32, 1)


def hot_rows(rows_of, entries):
    count, columns = rows_of.shape
    lane = iota((count, entries), 1)
    return jnp.concatenate(
        [
            jnp.where(rows_of[:, j : j + 1] == lane, 1.0, 0.0).astype(BF16)
            for j in range(columns)
        ],
        axis=0,
    )


def pick_rows(hot, table):
    got = mxu(hot, jnp.concatenate(split(table), axis=1))
    return got[:, :LANES] + got[:, LANES:]


def by_column(tiles, columns):
    block = iota((GROUP, LANES), 1) // RANK
    per = LANES // RANK
    rows = []
    for c in range(columns):
        pieces = []
        for first in range(0, len(tiles), per):
            piece = None
            for k in range(per):
                shift = ((k - c) * RANK) % LANES
                tile = tiles[first + k]
                moved = pltpu.roll(tile, shift, 1) if shift else tile
                piece = moved if piece is None else jnp.where(block == k, moved, piece)
            pieces.append(piece)
        rows.append(jnp.concatenate(pieces, axis=1))
    return jnp.concatenate(rows, axis=0)


def fetch(sources, targets, sems):
    copies = [
        pltpu.make_async_copy(source, target, sems.at[i])
        for i, (source, target) in enumerate(zip(sources, targets))
    ]
    for copy in copies:
        copy.start()
    return copies


def up_kernel(x_in, basis_in, up_in, leaves_in, counts_in, send_ref, *scratch):
    x_ref, basis_ref, up_ref, leaves_ref, counts_ref, sems = scratch
    for copy in fetch((x_in, basis_in, up_in, leaves_in, counts_in), scratch[:5], sems):
        copy.wait()
    columns = x_ref.shape[0]
    leaf_count = x_ref.shape[1] // PTS
    slots, peers = leaves_ref.shape
    wide = GROUP * PTS
    own = iota((GROUP, wide), 1) // PTS == iota((GROUP, wide), 0)
    lane_block = iota((GROUP, LANES), 1) // RANK
    diagonal = iota((columns * GROUP, GROUP * RANK), 1) // RANK == (
        iota((columns * GROUP, GROUP * RANK), 0) % GROUP
    )
    narrow = GROUP * RANK
    tiles = []
    for q in range(leaf_count // GROUP):
        x = x_ref[:, q * wide : (q + 1) * wide]
        spread = jnp.concatenate(
            [jnp.where(own, x[c : c + 1], 0.0) for c in range(columns)], axis=0
        )
        tiles.append(dot3(spread, basis_ref[:, q * wide : (q + 1) * wide], NT))
    lifted = [
        dot3(tile, up_ref[:, q * narrow : (q + 1) * narrow]) for q, tile in enumerate(tiles)
    ]
    skeleton = jnp.concatenate(
        [
            jnp.concatenate(
                [tile[c * GROUP : (c + 1) * GROUP] for c in range(columns)], axis=1
            )
            for tile in tiles
        ],
        axis=0,
    )
    parents = []
    for value in lifted:
        value = fold(jnp.where(diagonal, value, 0.0))
        total = None
        for c in range(columns):
            part = jnp.where(lane_block == c, value[c * GROUP : (c + 1) * GROUP], 0.0)
            total = part if total is None else total + part
        parents.append(jnp.sum(total, axis=0, keepdims=True))
    parents = jnp.concatenate(parents, axis=0)

    wanted = jnp.where(
        iota((slots, peers), 0) < counts_ref[...], leaves_ref[...].astype(F32), -1.0
    )
    rows = peers * slots
    expand = jnp.where(iota((rows, peers), 0) // slots == iota((rows, peers), 1), 1.0, 0.0)
    wanted = mxu(expand.astype(BF16), wanted.astype(BF16), NT)
    wanted = jnp.sum(
        jnp.where(iota((rows, slots), 0) % slots == iota((rows, slots), 1), wanted, 0.0),
        axis=1,
        keepdims=True,
    )
    hot = jnp.where(wanted == iota((rows, leaf_count), 1).astype(F32), 1.0, 0.0).astype(BF16)
    high, low = split(skeleton)
    got = mxu(hot, jnp.concatenate([high, low], axis=1))
    got = got[:, :LANES] + got[:, LANES:]
    send_ref[:, :slots, :] = got.reshape(peers, slots, LANES)
    par_count = parents.shape[0]
    send_ref[:, slots:, :] = jnp.broadcast_to(parents[None], (peers, par_count, LANES))


def pick_kernel(list_in, own_ref, left_ref, right_ref, *rest):
    outs, (table, places_ref, list_ref, sems) = rest[:-4], rest[-4:]
    columns, points = own_ref.shape
    leaf_count = points // PTS
    groups = len(outs)
    share = list_ref.shape[0] // groups
    blocks = 3 * points // LANES
    tile = list_in[...] - (lax.axis_index("leaf") - 1) * leaf_count
    turned = (tile + iota(tile.shape, 0)) & 1
    places_ref[...] = (tile >> 1) + turned * blocks
    copies = fetch((places_ref,), (list_ref,), sems)
    me = lax.axis_index("vec")
    for place, ref in enumerate((left_ref, own_ref, right_ref)):
        for b in range(points // LANES):
            tile = ref[:, b * LANES : (b + 1) * LANES]
            tile = jnp.concatenate([tile, tile], axis=0)
            at = place * (points // LANES) + b
            table[at] = tile
            table[blocks + at] = pltpu.roll(tile, PTS, 1)
    lower = iota((2 * columns, LANES), 1) < PTS
    upper_rows = iota((2 * columns, LANES), 0) >= columns
    for copy in copies:
        copy.wait()
    for s, out in enumerate(outs):
        first = lax.rem(me + s, groups) * share
        for pair in range(leaf_count // 2):
            halves = []
            for t in (2 * pair, 2 * pair + 1):
                halves.append(
                    jnp.where(lower, table[list_ref[first, t]], table[list_ref[first + 1, t]])
                )
            out[pair] = jnp.where(upper_rows, halves[1], halves[0])


def near_kernel(blocks_in, *rest):
    blocks_ref, sems = rest[-2:]
    copies = fetch((blocks_in,), (blocks_ref,), sems)
    groups = (len(rest) - 2) // 2
    parts, outs = rest[:groups], rest[groups : 2 * groups]
    columns, points = outs[0].shape
    share = blocks_ref.shape[0]
    lower = iota((columns, LANES), 1) < PTS
    rows = 2 * columns
    per = 2
    for copy in copies:
        copy.wait()
    for g in range(points // (per * LANES)):
        sources = jnp.concatenate(
            [part[g * per + h] for h in range(per) for part in parts], axis=0
        )
        block = blocks_ref[:, :, g * per * LANES : (g + 1) * per * LANES]
        value = dot3(sources, block.reshape(share * PTS, per * LANES))
        for h in range(per):
            for s, out in enumerate(outs):
                at = (h * groups + s) * rows
                tile = value[at : at + rows, h * LANES : (h + 1) * LANES]
                out[:, (g * per + h) * LANES : (g * per + h + 1) * LANES] = jnp.where(
                    lower, tile[:columns], tile[columns:]
                )


def far_kernel(*refs):
    recv_ref, sources, out_ref, targets, (hot_ref, sems) = (
        refs[0],
        refs[1:6],
        refs[6],
        refs[7:12],
        refs[12:],
    )
    top_ref, slot_ref, top_coupling_ref, down_ref, coupling_ref = targets
    coupling_in = sources[4]
    par_count, rows = out_ref.shape[:2]
    columns = rows // GROUP
    leaf_count = par_count * GROUP
    peers = recv_ref.shape[0]
    slots = recv_ref.shape[1] - par_count
    far_count = coupling_ref.shape[0]
    top_count = top_coupling_ref.shape[0]
    narrow = GROUP * RANK
    groups = range(par_count)

    def lanes(g, size):
        return slice(g * size, (g + 1) * size)

    copies = [
        pltpu.make_async_copy(sources[i], targets[i], sems.at[i]) for i in range(4)
    ]
    copies += [
        pltpu.make_async_copy(
            coupling_in.at[:, :, lanes(g, narrow)],
            coupling_ref.at[:, :, lanes(g, narrow)],
            sems.at[4 + g],
        )
        for g in groups
    ]
    for copy in copies:
        copy.start()
    diagonal = iota((rows, narrow), 1) // RANK == iota((rows, narrow), 0) % GROUP

    copies[0].wait()
    copies[1].wait()
    square = iota((leaf_count, leaf_count), 0) == iota((leaf_count, leaf_count), 1)
    square = jnp.where(square, 1.0, 0.0).astype(BF16)
    slot = slot_ref[...]
    slot = mxu(square, (slot >> 5).astype(F32).astype(BF16), NT) * 32.0 + mxu(
        square, (slot & 31).astype(F32).astype(BF16), NT
    )
    hot_top = hot_rows(top_ref[...], peers * par_count)
    hot_ref[...] = hot_rows(slot.astype(jnp.int32), peers * slots)
    tops = recv_ref[:, slots:, :].reshape(peers * par_count, LANES)
    top_got = pick_rows(hot_top, tops)
    tiles = recv_ref[:, :slots, :].reshape(peers * slots, LANES)
    got = pick_rows(hot_ref[...], tiles)

    for copy in copies[2:4]:
        copy.wait()
    field = dot3(
        by_column([top_got[lanes(j, GROUP)] for j in range(top_count)], columns),
        top_coupling_ref[...].reshape(top_count * RANK, narrow),
    )
    field = fold(jnp.where(diagonal, field, 0.0))[:, :RANK]
    lowered = dot3(field, down_ref[...])

    gathered = [
        by_column(
            [got[lanes(j * par_count + g, GROUP)] for j in range(far_count)],
            columns,
        )
        for g in groups
    ]
    fields = []
    for g in groups:
        copies[4 + g].wait()
        fields.append(
            dot3(
                gathered[g],
                coupling_ref[:, :, lanes(g, narrow)].reshape(far_count * RANK, narrow),
            )
        )
    for g in groups:
        above = jnp.concatenate(
            [
                jnp.broadcast_to(
                    lowered[c * GROUP + g : c * GROUP + g + 1, lanes(g, narrow)], (GROUP, narrow)
                )
                for c in range(columns)
            ],
            axis=0,
        )
        out_ref[g] = fold(jnp.where(diagonal, fields[g] + above, 0.0))


def out_kernel(field_ref, basis_ref, *rest):
    sums, out_ref = rest[:-1], rest[-1]
    columns = out_ref.shape[0]
    par_count, rows = field_ref.shape[:2]
    wide = GROUP * PTS
    diagonal = iota((rows, wide), 1) // PTS == iota((rows, wide), 0) % GROUP
    for g in range(par_count):
        lanes = slice(g * wide, (g + 1) * wide)
        value = dot3(field_ref[g, :, :RANK], basis_ref[:, lanes])
        value = jnp.where(diagonal, value, 0.0)
        total = jnp.sum(value.reshape(columns, GROUP, wide), axis=1)
        for part in sums:
            total = total + part[:, lanes]
        out_ref[:, lanes] = total


VMEM = pl.BlockSpec(memory_space=pltpu.VMEM)
ANY = pl.BlockSpec(memory_space=pl.ANY)
MIB = 1024 * 1024
UP_MIB, PICK_MIB, NEAR_MIB, FAR_MIB, OUT_MIB = 60, 24, 24, 51, 24
UP_US, PICK_US, NEAR_US, FAR_US, OUT_US = 2, 2, 8, 4, 1


def cost(micros):
    return pl.CostEstimate(flops=int(micros * 1e9), bytes_accessed=0, transcendentals=0)


def buffers(*arrays):
    return [pltpu.VMEM(array.shape, array.dtype) for array in arrays] + [
        pltpu.SemaphoreType.DMA((len(arrays),))
    ]


def local(
    points_x,
    near_list,
    near_blocks,
    leaf_basis,
    out_basis,
    up_transfer,
    down_transfer,
    send_leaves,
    send_counts,
    recv_slot,
    leaf_coupling,
    top_list,
    top_coupling,
):
    columns, points = points_x.shape
    leaf_count = near_list.shape[0]
    par_count = top_list.shape[0]
    peers, slots = send_leaves.shape[1:]
    groups = lax.axis_size("vec")
    ring = lax.axis_size("leaf")

    left = lax.ppermute(points_x, "leaf", [(i, (i + 1) % ring) for i in range(ring)])
    right = lax.ppermute(points_x, "leaf", [((i + 1) % ring, i) for i in range(ring)])

    up_args = (points_x, leaf_basis, up_transfer, send_leaves[0].T, send_counts)
    send = pl.pallas_call(
        up_kernel,
        name="up",
        out_shape=jax.ShapeDtypeStruct((peers, slots + par_count, LANES), F32),
        in_specs=[ANY] * 5,
        out_specs=VMEM,
        scratch_shapes=buffers(*up_args),
        compiler_params=pltpu.CompilerParams(vmem_limit_bytes=UP_MIB * MIB),
        cost_estimate=cost(UP_US),
    )(*up_args)
    recv = lax.all_to_all(send, "leaf", split_axis=0, concat_axis=0, tiled=True)

    picked = pl.pallas_call(
        pick_kernel,
        name="pick",
        out_shape=[jax.ShapeDtypeStruct((leaf_count // 2, 2 * columns, LANES), F32)] * groups,
        in_specs=[VMEM] * 4,
        out_specs=[VMEM] * groups,
        scratch_shapes=[
            pltpu.VMEM((2 * 3 * points // LANES, 2 * columns, LANES), F32),
            pltpu.VMEM(near_list.T.shape, jnp.int32),
            pltpu.SMEM(near_list.T.shape, jnp.int32),
            pltpu.SemaphoreType.DMA((1,)),
        ],
        compiler_params=pltpu.CompilerParams(vmem_limit_bytes=PICK_MIB * MIB),
        cost_estimate=cost(PICK_US),
    )(near_list.T, points_x, left, right)
    parts = [picked[0]] + [
        lax.ppermute(picked[s], "vec", [(i, (i + s) % groups) for i in range(groups)])
        for s in range(1, groups)
    ]

    partial = pl.pallas_call(
        near_kernel,
        name="near",
        out_shape=[jax.ShapeDtypeStruct((columns, points), F32)] * groups,
        in_specs=[ANY] + [VMEM] * groups,
        out_specs=[VMEM] * groups,
        scratch_shapes=buffers(near_blocks),
        compiler_params=pltpu.CompilerParams(vmem_limit_bytes=NEAR_MIB * MIB),
        cost_estimate=cost(NEAR_US),
    )(near_blocks, *parts)
    sums = [partial[0]] + [
        lax.ppermute(partial[s], "vec", [(i, (i - s) % groups) for i in range(groups)])
        for s in range(1, groups)
    ]
    far_args = [
        top_list,
        recv_slot.T,
        top_coupling,
        down_transfer,
        leaf_coupling,
    ]
    fields = pl.pallas_call(
        far_kernel,
        name="far",
        out_shape=jax.ShapeDtypeStruct((par_count, columns * GROUP, LANES), F32),
        in_specs=[VMEM] + [ANY] * len(far_args),
        out_specs=VMEM,
        scratch_shapes=[pltpu.VMEM(array.shape, array.dtype) for array in far_args]
        + [
            pltpu.VMEM((recv_slot.size, peers * slots), BF16),
            pltpu.SemaphoreType.DMA((len(far_args) + par_count,)),
        ],
        compiler_params=pltpu.CompilerParams(vmem_limit_bytes=FAR_MIB * MIB),
        cost_estimate=cost(FAR_US),
    )(recv, *far_args)
    return pl.pallas_call(
        out_kernel,
        name="out",
        out_shape=jax.ShapeDtypeStruct((columns, points), F32),
        in_specs=[VMEM] * (2 + groups),
        out_specs=VMEM,
        compiler_params=pltpu.CompilerParams(vmem_limit_bytes=OUT_MIB * MIB),
        cost_estimate=cost(OUT_US),
    )(fields, out_basis, *sums)


def solution(mesh):
    placed = (
        P("vec", "leaf"),
        P("leaf", None),
        P("vec", None, "leaf"),
        P(None, "leaf"),
        P(None, "leaf"),
        P(None, "leaf"),
        P(None, "leaf"),
        P("leaf", None, None),
        P("leaf", None),
        P("leaf", None),
        P(None, None, "leaf"),
        P("leaf", None),
        P(None, None, "leaf"),
    )
    return jax.shard_map(
        local, mesh=mesh, in_specs=placed, out_specs=P("vec", "leaf"), check_vma=False
    )
```

```python
import jax
import jax.numpy as jnp
from jax import lax
from jax.experimental import pallas as pl
from jax.experimental.pallas import tpu as pltpu
from jax.sharding import PartitionSpec as P

PTS = 64
RANK = 32
GROUP = 8
LANES = 128
F32 = jnp.float32
BF16 = jnp.bfloat16


def iota(shape, dim):
    return lax.broadcasted_iota(jnp.int32, shape, dim)


def split(value):
    high = value.astype(BF16)
    return high, (value - high.astype(F32)).astype(BF16)


NN = (((1,), (0,)), ((), ()))
NT = (((1,), (1,)), ((), ()))


def mxu(left, right, dims=NN):
    return lax.dot_general(left, right, dims, preferred_element_type=F32)


def dot3(left, right, dims=NN):
    rows = left.shape[0]
    left_high, left_low = split(left)
    right_high, right_low = right if isinstance(right, tuple) else split(right)
    both = mxu(jnp.concatenate([left_high, left_low], axis=0), right_high, dims)
    return both[:rows] + both[rows:] + mxu(left_high, right_low, dims)


def fold(value):
    value = value[:, :LANES] + value[:, LANES:]
    value = value + pltpu.roll(value, 64, 1)
    return value + pltpu.roll(value, 32, 1)


def hot_rows(rows_of, entries):
    count, columns = rows_of.shape
    lane = iota((count, entries), 1)
    return jnp.concatenate(
        [
            jnp.where(rows_of[:, j : j + 1] == lane, 1.0, 0.0).astype(BF16)
            for j in range(columns)
        ],
        axis=0,
    )


def pick_rows(hot, table):
    got = mxu(hot, jnp.concatenate(split(table), axis=1))
    return got[:, :LANES] + got[:, LANES:]


def by_column(tiles, columns):
    block = iota((GROUP, LANES), 1) // RANK
    per = LANES // RANK
    rows = []
    for c in range(columns):
        pieces = []
        for first in range(0, len(tiles), per):
            piece = None
            for k in range(per):
                shift = ((k - c) * RANK) % LANES
                tile = tiles[first + k]
                moved = pltpu.roll(tile, shift, 1) if shift else tile
                piece = moved if piece is None else jnp.where(block == k, moved, piece)
            pieces.append(piece)
        rows.append(jnp.concatenate(pieces, axis=1))
    return jnp.concatenate(rows, axis=0)


def fetch(sources, targets, sems):
    copies = [
        pltpu.make_async_copy(source, target, sems.at[i])
        for i, (source, target) in enumerate(zip(sources, targets))
    ]
    for copy in copies:
        copy.start()
    return copies


def up_kernel(x_in, basis_in, up_in, leaves_in, counts_in, send_ref, *scratch):
    x_ref, basis_ref, up_ref, leaves_ref, counts_ref, sems = scratch
    for copy in fetch((x_in, basis_in, up_in, leaves_in, counts_in), scratch[:5], sems):
        copy.wait()
    columns = x_ref.shape[0]
    leaf_count = x_ref.shape[1] // PTS
    slots, peers = leaves_ref.shape
    wide = GROUP * PTS
    own = iota((GROUP, wide), 1) // PTS == iota((GROUP, wide), 0)
    lane_block = iota((GROUP, LANES), 1) // RANK
    diagonal = iota((columns * GROUP, GROUP * RANK), 1) // RANK == (
        iota((columns * GROUP, GROUP * RANK), 0) % GROUP
    )
    narrow = GROUP * RANK
    tiles = []
    for q in range(leaf_count // GROUP):
        x = x_ref[:, q * wide : (q + 1) * wide]
        spread = jnp.concatenate(
            [jnp.where(own, x[c : c + 1], 0.0) for c in range(columns)], axis=0
        )
        tiles.append(dot3(spread, basis_ref[:, q * wide : (q + 1) * wide], NT))
    lifted = [
        dot3(tile, up_ref[:, q * narrow : (q + 1) * narrow]) for q, tile in enumerate(tiles)
    ]
    skeleton = jnp.concatenate(
        [
            jnp.concatenate(
                [tile[c * GROUP : (c + 1) * GROUP] for c in range(columns)], axis=1
            )
            for tile in tiles
        ],
        axis=0,
    )
    parents = []
    for value in lifted:
        value = fold(jnp.where(diagonal, value, 0.0))
        total = None
        for c in range(columns):
            part = jnp.where(lane_block == c, value[c * GROUP : (c + 1) * GROUP], 0.0)
            total = part if total is None else total + part
        parents.append(jnp.sum(total, axis=0, keepdims=True))
    parents = jnp.concatenate(parents, axis=0)

    wanted = jnp.where(
        iota((slots, peers), 0) < counts_ref[...], leaves_ref[...].astype(F32), -1.0
    )
    rows = peers * slots
    expand = jnp.where(iota((rows, peers), 0) // slots == iota((rows, peers), 1), 1.0, 0.0)
    wanted = mxu(expand.astype(BF16), wanted.astype(BF16), NT)
    wanted = jnp.sum(
        jnp.where(iota((rows, slots), 0) % slots == iota((rows, slots), 1), wanted, 0.0),
        axis=1,
        keepdims=True,
    )
    hot = jnp.where(wanted == iota((rows, leaf_count), 1).astype(F32), 1.0, 0.0).astype(BF16)
    high, low = split(skeleton)
    got = mxu(hot, jnp.concatenate([high, low], axis=1))
    got = got[:, :LANES] + got[:, LANES:]
    send_ref[:, :slots, :] = got.reshape(peers, slots, LANES)
    par_count = parents.shape[0]
    send_ref[:, slots:, :] = jnp.broadcast_to(parents[None], (peers, par_count, LANES))


def pick_kernel(list_in, own_ref, left_ref, right_ref, *rest):
    outs, (table, places_ref, list_ref, sems) = rest[:-4], rest[-4:]
    columns, points = own_ref.shape
    leaf_count = points // PTS
    groups = len(outs)
    share = list_ref.shape[0] // groups
    blocks = 3 * points // LANES
    tile = list_in[...] - (lax.axis_index("leaf") - 1) * leaf_count
    turned = (tile + iota(tile.shape, 0)) & 1
    places_ref[...] = (tile >> 1) + turned * blocks
    copies = fetch((places_ref,), (list_ref,), sems)
    me = lax.axis_index("vec")
    for place, ref in enumerate((left_ref, own_ref, right_ref)):
        for b in range(points // LANES):
            tile = ref[:, b * LANES : (b + 1) * LANES]
            tile = jnp.concatenate([tile, tile], axis=0)
            at = place * (points // LANES) + b
            table[at] = tile
            table[blocks + at] = pltpu.roll(tile, PTS, 1)
    lower = iota((2 * columns, LANES), 1) < PTS
    upper_rows = iota((2 * columns, LANES), 0) >= columns
    for copy in copies:
        copy.wait()
    for s, out in enumerate(outs):
        first = lax.rem(me + s, groups) * share
        for pair in range(leaf_count // 2):
            halves = []
            for t in (2 * pair, 2 * pair + 1):
                halves.append(
                    jnp.where(lower, table[list_ref[first, t]], table[list_ref[first + 1, t]])
                )
            out[pair] = jnp.where(upper_rows, halves[1], halves[0])


def near_kernel(blocks_in, *rest):
    blocks_ref, sems = rest[-2:]
    copies = fetch((blocks_in,), (blocks_ref,), sems)
    groups = (len(rest) - 2) // 2
    parts, outs = rest[:groups], rest[groups : 2 * groups]
    columns, points = outs[0].shape
    share = blocks_ref.shape[0]
    lower = iota((columns, LANES), 1) < PTS
    rows = 2 * columns
    per = 2
    for copy in copies:
        copy.wait()
    for g in range(points // (per * LANES)):
        sources = jnp.concatenate(
            [part[g * per + h] for h in range(per) for part in parts], axis=0
        )
        block = blocks_ref[:, :, g * per * LANES : (g + 1) * per * LANES]
        value = dot3(sources, block.reshape(share * PTS, per * LANES))
        for h in range(per):
            for s, out in enumerate(outs):
                at = (h * groups + s) * rows
                tile = value[at : at + rows, h * LANES : (h + 1) * LANES]
                out[:, (g * per + h) * LANES : (g * per + h + 1) * LANES] = jnp.where(
                    lower, tile[:columns], tile[columns:]
                )


def far_kernel(*refs):
    recv_ref, sources, out_ref, targets, (hot_ref, sems) = (
        refs[0],
        refs[1:6],
        refs[6],
        refs[7:12],
        refs[12:],
    )
    top_ref, slot_ref, top_coupling_ref, down_ref, coupling_ref = targets
    coupling_in = sources[4]
    par_count, rows = out_ref.shape[:2]
    columns = rows // GROUP
    leaf_count = par_count * GROUP
    peers = recv_ref.shape[0]
    slots = recv_ref.shape[1] - par_count
    far_count = coupling_ref.shape[0]
    top_count = top_coupling_ref.shape[0]
    narrow = GROUP * RANK
    groups = range(par_count)

    def lanes(g, size):
        return slice(g * size, (g + 1) * size)

    copies = [
        pltpu.make_async_copy(sources[i], targets[i], sems.at[i]) for i in range(4)
    ]
    copies += [
        pltpu.make_async_copy(
            coupling_in.at[:, :, lanes(g, 2 * narrow)],
            coupling_ref.at[:, :, lanes(g, 2 * narrow)],
            sems.at[4 + g],
        )
        for g in range(par_count // 2)
    ]
    for copy in copies:
        copy.start()
    diagonal = iota((rows, narrow), 1) // RANK == iota((rows, narrow), 0) % GROUP

    copies[0].wait()
    copies[1].wait()
    square = iota((leaf_count, leaf_count), 0) == iota((leaf_count, leaf_count), 1)
    square = jnp.where(square, 1.0, 0.0).astype(BF16)
    slot = slot_ref[...]
    slot = mxu(square, (slot >> 5).astype(F32).astype(BF16), NT) * 32.0 + mxu(
        square, (slot & 31).astype(F32).astype(BF16), NT
    )
    hot_top = hot_rows(top_ref[...], peers * par_count)
    hot_ref[...] = hot_rows(slot.astype(jnp.int32), peers * slots)
    tops = recv_ref[:, slots:, :].reshape(peers * par_count, LANES)
    top_got = pick_rows(hot_top, tops)
    tiles = recv_ref[:, :slots, :].reshape(peers * slots, LANES)
    got = pick_rows(hot_ref[...], tiles)

    for copy in copies[2:4]:
        copy.wait()
    field = dot3(
        by_column([top_got[lanes(j, GROUP)] for j in range(top_count)], columns),
        top_coupling_ref[...].reshape(top_count * RANK, narrow),
    )
    field = fold(jnp.where(diagonal, field, 0.0))[:, :RANK]
    lowered = dot3(field, down_ref[...])

    gathered = [
        by_column(
            [got[lanes(j * par_count + g, GROUP)] for j in range(far_count)],
            columns,
        )
        for g in groups
    ]
    fields = []
    for g in groups:
        if g % 2 == 0:
            copies[4 + g // 2].wait()
        fields.append(
            dot3(
                gathered[g],
                coupling_ref[:, :, lanes(g, narrow)].reshape(far_count * RANK, narrow),
            )
        )
    for g in groups:
        above = jnp.concatenate(
            [
                jnp.broadcast_to(
                    lowered[c * GROUP + g : c * GROUP + g + 1, lanes(g, narrow)], (GROUP, narrow)
                )
                for c in range(columns)
            ],
            axis=0,
        )
        out_ref[g] = fold(jnp.where(diagonal, fields[g] + above, 0.0))


def out_kernel(field_ref, basis_ref, *rest):
    sums, out_ref = rest[:-1], rest[-1]
    columns = out_ref.shape[0]
    par_count, rows = field_ref.shape[:2]
    wide = GROUP * PTS
    diagonal = iota((rows, wide), 1) // PTS == iota((rows, wide), 0) % GROUP
    for g in range(par_count):
        lanes = slice(g * wide, (g + 1) * wide)
        value = dot3(field_ref[g, :, :RANK], basis_ref[:, lanes])
        value = jnp.where(diagonal, value, 0.0)
        total = jnp.sum(value.reshape(columns, GROUP, wide), axis=1)
        for part in sums:
            total = total + part[:, lanes]
        out_ref[:, lanes] = total


VMEM = pl.BlockSpec(memory_space=pltpu.VMEM)
ANY = pl.BlockSpec(memory_space=pl.ANY)
MIB = 1024 * 1024
UP_MIB, PICK_MIB, NEAR_MIB, FAR_MIB, OUT_MIB = 60, 24, 24, 51, 24
UP_US, PICK_US, NEAR_US, FAR_US, OUT_US = 2, 2, 8, 4, 1


def cost(micros):
    return pl.CostEstimate(flops=int(micros * 1e9), bytes_accessed=0, transcendentals=0)


def buffers(*arrays):
    return [pltpu.VMEM(array.shape, array.dtype) for array in arrays] + [
        pltpu.SemaphoreType.DMA((len(arrays),))
    ]


def local(
    points_x,
    near_list,
    near_blocks,
    leaf_basis,
    out_basis,
    up_transfer,
    down_transfer,
    send_leaves,
    send_counts,
    recv_slot,
    leaf_coupling,
    top_list,
    top_coupling,
):
    columns, points = points_x.shape
    leaf_count = near_list.shape[0]
    par_count = top_list.shape[0]
    peers, slots = send_leaves.shape[1:]
    groups = lax.axis_size("vec")
    ring = lax.axis_size("leaf")

    left = lax.ppermute(points_x, "leaf", [(i, (i + 1) % ring) for i in range(ring)])
    right = lax.ppermute(points_x, "leaf", [((i + 1) % ring, i) for i in range(ring)])

    up_args = (points_x, leaf_basis, up_transfer, send_leaves[0].T, send_counts)
    send = pl.pallas_call(
        up_kernel,
        name="up",
        out_shape=jax.ShapeDtypeStruct((peers, slots + par_count, LANES), F32),
        in_specs=[ANY] * 5,
        out_specs=VMEM,
        scratch_shapes=buffers(*up_args),
        compiler_params=pltpu.CompilerParams(vmem_limit_bytes=UP_MIB * MIB),
        cost_estimate=cost(UP_US),
    )(*up_args)
    recv = lax.all_to_all(send, "leaf", split_axis=0, concat_axis=0, tiled=True)

    picked = pl.pallas_call(
        pick_kernel,
        name="pick",
        out_shape=[jax.ShapeDtypeStruct((leaf_count // 2, 2 * columns, LANES), F32)] * groups,
        in_specs=[VMEM] * 4,
        out_specs=[VMEM] * groups,
        scratch_shapes=[
            pltpu.VMEM((2 * 3 * points // LANES, 2 * columns, LANES), F32),
            pltpu.VMEM(near_list.T.shape, jnp.int32),
            pltpu.SMEM(near_list.T.shape, jnp.int32),
            pltpu.SemaphoreType.DMA((1,)),
        ],
        compiler_params=pltpu.CompilerParams(vmem_limit_bytes=PICK_MIB * MIB),
        cost_estimate=cost(PICK_US),
    )(near_list.T, points_x, left, right)
    parts = [picked[0]] + [
        lax.ppermute(picked[s], "vec", [(i, (i + s) % groups) for i in range(groups)])
        for s in range(1, groups)
    ]

    partial = pl.pallas_call(
        near_kernel,
        name="near",
        out_shape=[jax.ShapeDtypeStruct((columns, points), F32)] * groups,
        in_specs=[ANY] + [VMEM] * groups,
        out_specs=[VMEM] * groups,
        scratch_shapes=buffers(near_blocks),
        compiler_params=pltpu.CompilerParams(vmem_limit_bytes=NEAR_MIB * MIB),
        cost_estimate=cost(NEAR_US),
    )(near_blocks, *parts)
    sums = [partial[0]] + [
        lax.ppermute(partial[s], "vec", [(i, (i - s) % groups) for i in range(groups)])
        for s in range(1, groups)
    ]
    far_args = [
        top_list,
        recv_slot.T,
        top_coupling,
        down_transfer,
        leaf_coupling,
    ]
    fields = pl.pallas_call(
        far_kernel,
        name="far",
        out_shape=jax.ShapeDtypeStruct((par_count, columns * GROUP, LANES), F32),
        in_specs=[VMEM] + [ANY] * len(far_args),
        out_specs=VMEM,
        scratch_shapes=[pltpu.VMEM(array.shape, array.dtype) for array in far_args]
        + [
            pltpu.VMEM((recv_slot.size, peers * slots), BF16),
            pltpu.SemaphoreType.DMA((len(far_args) + par_count,)),
        ],
        compiler_params=pltpu.CompilerParams(vmem_limit_bytes=FAR_MIB * MIB),
        cost_estimate=cost(FAR_US),
    )(recv, *far_args)
    return pl.pallas_call(
        out_kernel,
        name="out",
        out_shape=jax.ShapeDtypeStruct((columns, points), F32),
        in_specs=[VMEM] * (2 + groups),
        out_specs=VMEM,
        compiler_params=pltpu.CompilerParams(vmem_limit_bytes=OUT_MIB * MIB),
        cost_estimate=cost(OUT_US),
    )(fields, out_basis, *sums)


def solution(mesh):
    placed = (
        P("vec", "leaf"),
        P("leaf", None),
        P("vec", None, "leaf"),
        P(None, "leaf"),
        P(None, "leaf"),
        P(None, "leaf"),
        P(None, "leaf"),
        P("leaf", None, None),
        P("leaf", None),
        P("leaf", None),
        P(None, None, "leaf"),
        P("leaf", None),
        P(None, None, "leaf"),
    )
    return jax.shard_map(
        local, mesh=mesh, in_specs=placed, out_specs=P("vec", "leaf"), check_vma=False
    )
```

```python
import jax
import jax.numpy as jnp
from jax import lax
from jax.experimental import pallas as pl
from jax.experimental.pallas import tpu as pltpu
from jax.sharding import PartitionSpec as P

PTS = 64
RANK = 32
GROUP = 8
LANES = 128
F32 = jnp.float32
BF16 = jnp.bfloat16


def iota(shape, dim):
    return lax.broadcasted_iota(jnp.int32, shape, dim)


def split(value):
    high = value.astype(BF16)
    return high, (value - high.astype(F32)).astype(BF16)


NN = (((1,), (0,)), ((), ()))
NT = (((1,), (1,)), ((), ()))


def mxu(left, right, dims=NN):
    return lax.dot_general(left, right, dims, preferred_element_type=F32)


def dot3(left, right, dims=NN):
    rows = left.shape[0]
    left_high, left_low = split(left)
    right_high, right_low = right if isinstance(right, tuple) else split(right)
    both = mxu(jnp.concatenate([left_high, left_low], axis=0), right_high, dims)
    return both[:rows] + both[rows:] + mxu(left_high, right_low, dims)


def fold(value):
    value = value[:, :LANES] + value[:, LANES:]
    value = value + pltpu.roll(value, 64, 1)
    return value + pltpu.roll(value, 32, 1)


def hot_rows(rows_of, entries):
    count, columns = rows_of.shape
    lane = iota((count, entries), 1)
    return jnp.concatenate(
        [
            jnp.where(rows_of[:, j : j + 1] == lane, 1.0, 0.0).astype(BF16)
            for j in range(columns)
        ],
        axis=0,
    )


def pick_rows(hot, table):
    got = mxu(hot, jnp.concatenate(split(table), axis=1))
    return got[:, :LANES] + got[:, LANES:]


def by_column(tiles, columns):
    block = iota((GROUP, LANES), 1) // RANK
    per = LANES // RANK
    rows = []
    for c in range(columns):
        pieces = []
        for first in range(0, len(tiles), per):
            piece = None
            for k in range(per):
                shift = ((k - c) * RANK) % LANES
                tile = tiles[first + k]
                moved = pltpu.roll(tile, shift, 1) if shift else tile
                piece = moved if piece is None else jnp.where(block == k, moved, piece)
            pieces.append(piece)
        rows.append(jnp.concatenate(pieces, axis=1))
    return jnp.concatenate(rows, axis=0)


def fetch(sources, targets, sems):
    copies = [
        pltpu.make_async_copy(source, target, sems.at[i])
        for i, (source, target) in enumerate(zip(sources, targets))
    ]
    for copy in copies:
        copy.start()
    return copies


def up_kernel(x_in, basis_in, up_in, leaves_in, counts_in, send_ref, *scratch):
    x_ref, basis_ref, up_ref, leaves_ref, counts_ref, sems = scratch
    half = basis_in.shape[1] // 2
    left, right = (slice(None), slice(0, half)), (slice(None), slice(half, 2 * half))
    for copy in fetch(
        (basis_in.at[left], basis_in.at[right], x_in, up_in, leaves_in, counts_in),
        (basis_ref.at[left], basis_ref.at[right], x_ref, up_ref, leaves_ref, counts_ref),
        sems,
    ):
        copy.wait()
    columns = x_ref.shape[0]
    leaf_count = x_ref.shape[1] // PTS
    slots, peers = leaves_ref.shape
    wide = GROUP * PTS
    own = iota((GROUP, wide), 1) // PTS == iota((GROUP, wide), 0)
    lane_block = iota((GROUP, LANES), 1) // RANK
    diagonal = iota((columns * GROUP, GROUP * RANK), 1) // RANK == (
        iota((columns * GROUP, GROUP * RANK), 0) % GROUP
    )
    narrow = GROUP * RANK
    tiles = []
    for q in range(leaf_count // GROUP):
        x = x_ref[:, q * wide : (q + 1) * wide]
        spread = jnp.concatenate(
            [jnp.where(own, x[c : c + 1], 0.0) for c in range(columns)], axis=0
        )
        tiles.append(dot3(spread, basis_ref[:, q * wide : (q + 1) * wide], NT))
    lifted = [
        dot3(tile, up_ref[:, q * narrow : (q + 1) * narrow]) for q, tile in enumerate(tiles)
    ]
    skeleton = jnp.concatenate(
        [
            jnp.concatenate(
                [tile[c * GROUP : (c + 1) * GROUP] for c in range(columns)], axis=1
            )
            for tile in tiles
        ],
        axis=0,
    )
    parents = []
    for value in lifted:
        value = fold(jnp.where(diagonal, value, 0.0))
        total = None
        for c in range(columns):
            part = jnp.where(lane_block == c, value[c * GROUP : (c + 1) * GROUP], 0.0)
            total = part if total is None else total + part
        parents.append(jnp.sum(total, axis=0, keepdims=True))
    parents = jnp.concatenate(parents, axis=0)

    wanted = jnp.where(
        iota((slots, peers), 0) < counts_ref[...], leaves_ref[...].astype(F32), -1.0
    )
    rows = peers * slots
    expand = jnp.where(iota((rows, peers), 0) // slots == iota((rows, peers), 1), 1.0, 0.0)
    wanted = mxu(expand.astype(BF16), wanted.astype(BF16), NT)
    wanted = jnp.sum(
        jnp.where(iota((rows, slots), 0) % slots == iota((rows, slots), 1), wanted, 0.0),
        axis=1,
        keepdims=True,
    )
    hot = jnp.where(wanted == iota((rows, leaf_count), 1).astype(F32), 1.0, 0.0).astype(BF16)
    high, low = split(skeleton)
    got = mxu(hot, jnp.concatenate([high, low], axis=1))
    got = got[:, :LANES] + got[:, LANES:]
    send_ref[:, :slots, :] = got.reshape(peers, slots, LANES)
    par_count = parents.shape[0]
    send_ref[:, slots:, :] = jnp.broadcast_to(parents[None], (peers, par_count, LANES))


def pick_kernel(list_in, own_ref, left_ref, right_ref, *rest):
    outs, (table, places_ref, list_ref, sems) = rest[:-4], rest[-4:]
    columns, points = own_ref.shape
    leaf_count = points // PTS
    groups = len(outs)
    share = list_ref.shape[0] // groups
    blocks = 3 * points // LANES
    tile = list_in[...] - (lax.axis_index("leaf") - 1) * leaf_count
    turned = (tile + iota(tile.shape, 0)) & 1
    places_ref[...] = (tile >> 1) + turned * blocks
    copies = fetch((places_ref,), (list_ref,), sems)
    me = lax.axis_index("vec")
    for place, ref in enumerate((left_ref, own_ref, right_ref)):
        for b in range(points // LANES):
            tile = ref[:, b * LANES : (b + 1) * LANES]
            tile = jnp.concatenate([tile, tile], axis=0)
            at = place * (points // LANES) + b
            table[at] = tile
            table[blocks + at] = pltpu.roll(tile, PTS, 1)
    lower = iota((2 * columns, LANES), 1) < PTS
    upper_rows = iota((2 * columns, LANES), 0) >= columns
    for copy in copies:
        copy.wait()
    for s, out in enumerate(outs):
        first = lax.rem(me + s, groups) * share
        for pair in range(leaf_count // 2):
            halves = []
            for t in (2 * pair, 2 * pair + 1):
                halves.append(
                    jnp.where(lower, table[list_ref[first, t]], table[list_ref[first + 1, t]])
                )
            out[pair] = jnp.where(upper_rows, halves[1], halves[0])


def near_kernel(blocks_in, *rest):
    blocks_ref, sems = rest[-2:]
    copies = fetch((blocks_in,), (blocks_ref,), sems)
    groups = (len(rest) - 2) // 2
    parts, outs = rest[:groups], rest[groups : 2 * groups]
    columns, points = outs[0].shape
    share = blocks_ref.shape[0]
    lower = iota((columns, LANES), 1) < PTS
    rows = 2 * columns
    per = 2
    for copy in copies:
        copy.wait()
    for g in range(points // (per * LANES)):
        sources = jnp.concatenate(
            [part[g * per + h] for h in range(per) for part in parts], axis=0
        )
        block = blocks_ref[:, :, g * per * LANES : (g + 1) * per * LANES]
        value = dot3(sources, block.reshape(share * PTS, per * LANES))
        for h in range(per):
            for s, out in enumerate(outs):
                at = (h * groups + s) * rows
                tile = value[at : at + rows, h * LANES : (h + 1) * LANES]
                out[:, (g * per + h) * LANES : (g * per + h + 1) * LANES] = jnp.where(
                    lower, tile[:columns], tile[columns:]
                )


def far_kernel(*refs):
    recv_ref, sources, out_ref, targets, (hot_ref, sems) = (
        refs[0],
        refs[1:6],
        refs[6],
        refs[7:12],
        refs[12:],
    )
    top_ref, slot_ref, top_coupling_ref, down_ref, coupling_ref = targets
    coupling_in = sources[4]
    par_count, rows = out_ref.shape[:2]
    columns = rows // GROUP
    leaf_count = par_count * GROUP
    peers = recv_ref.shape[0]
    slots = recv_ref.shape[1] - par_count
    far_count = coupling_ref.shape[0]
    top_count = top_coupling_ref.shape[0]
    narrow = GROUP * RANK
    groups = range(par_count)

    def lanes(g, size):
        return slice(g * size, (g + 1) * size)

    copies = [
        pltpu.make_async_copy(sources[i], targets[i], sems.at[i]) for i in range(4)
    ]
    copies += [
        pltpu.make_async_copy(
            coupling_in.at[:, :, lanes(g, 2 * narrow)],
            coupling_ref.at[:, :, lanes(g, 2 * narrow)],
            sems.at[4 + g],
        )
        for g in range(par_count // 2)
    ]
    for copy in copies:
        copy.start()
    diagonal = iota((rows, narrow), 1) // RANK == iota((rows, narrow), 0) % GROUP

    copies[0].wait()
    copies[1].wait()
    square = iota((leaf_count, leaf_count), 0) == iota((leaf_count, leaf_count), 1)
    square = jnp.where(square, 1.0, 0.0).astype(BF16)
    slot = slot_ref[...]
    slot = mxu(square, (slot >> 5).astype(F32).astype(BF16), NT) * 32.0 + mxu(
        square, (slot & 31).astype(F32).astype(BF16), NT
    )
    hot_top = hot_rows(top_ref[...], peers * par_count)
    hot_ref[...] = hot_rows(slot.astype(jnp.int32), peers * slots)
    tops = recv_ref[:, slots:, :].reshape(peers * par_count, LANES)
    top_got = pick_rows(hot_top, tops)
    tiles = recv_ref[:, :slots, :].reshape(peers * slots, LANES)
    got = pick_rows(hot_ref[...], tiles)

    for copy in copies[2:4]:
        copy.wait()
    field = dot3(
        by_column([top_got[lanes(j, GROUP)] for j in range(top_count)], columns),
        top_coupling_ref[...].reshape(top_count * RANK, narrow),
    )
    field = fold(jnp.where(diagonal, field, 0.0))[:, :RANK]
    lowered = dot3(field, down_ref[...])

    gathered = [
        by_column(
            [got[lanes(j * par_count + g, GROUP)] for j in range(far_count)],
            columns,
        )
        for g in groups
    ]
    fields = []
    for g in groups:
        if g % 2 == 0:
            copies[4 + g // 2].wait()
        fields.append(
            dot3(
                gathered[g],
                coupling_ref[:, :, lanes(g, narrow)].reshape(far_count * RANK, narrow),
            )
        )
    for g in groups:
        above = jnp.concatenate(
            [
                jnp.broadcast_to(
                    lowered[c * GROUP + g : c * GROUP + g + 1, lanes(g, narrow)], (GROUP, narrow)
                )
                for c in range(columns)
            ],
            axis=0,
        )
        out_ref[g] = fold(jnp.where(diagonal, fields[g] + above, 0.0))


def out_kernel(field_ref, basis_ref, *rest):
    sums, out_ref = rest[:-1], rest[-1]
    columns = out_ref.shape[0]
    par_count, rows = field_ref.shape[:2]
    wide = GROUP * PTS
    diagonal = iota((rows, wide), 1) // PTS == iota((rows, wide), 0) % GROUP
    for g in range(par_count):
        lanes = slice(g * wide, (g + 1) * wide)
        value = dot3(field_ref[g, :, :RANK], basis_ref[:, lanes])
        value = jnp.where(diagonal, value, 0.0)
        total = jnp.sum(value.reshape(columns, GROUP, wide), axis=1)
        for part in sums:
            total = total + part[:, lanes]
        out_ref[:, lanes] = total


VMEM = pl.BlockSpec(memory_space=pltpu.VMEM)
ANY = pl.BlockSpec(memory_space=pl.ANY)
MIB = 1024 * 1024
UP_MIB, PICK_MIB, NEAR_MIB, FAR_MIB, OUT_MIB = 60, 24, 24, 51, 24
UP_US, PICK_US, NEAR_US, FAR_US, OUT_US = 2, 2, 8, 4, 1


def cost(micros):
    return pl.CostEstimate(flops=int(micros * 1e9), bytes_accessed=0, transcendentals=0)


def buffers(*arrays):
    return [pltpu.VMEM(array.shape, array.dtype) for array in arrays] + [
        pltpu.SemaphoreType.DMA((len(arrays),))
    ]


def local(
    points_x,
    near_list,
    near_blocks,
    leaf_basis,
    out_basis,
    up_transfer,
    down_transfer,
    send_leaves,
    send_counts,
    recv_slot,
    leaf_coupling,
    top_list,
    top_coupling,
):
    columns, points = points_x.shape
    leaf_count = near_list.shape[0]
    par_count = top_list.shape[0]
    peers, slots = send_leaves.shape[1:]
    groups = lax.axis_size("vec")
    ring = lax.axis_size("leaf")

    left = lax.ppermute(points_x, "leaf", [(i, (i + 1) % ring) for i in range(ring)])
    right = lax.ppermute(points_x, "leaf", [((i + 1) % ring, i) for i in range(ring)])

    up_args = (points_x, leaf_basis, up_transfer, send_leaves[0].T, send_counts)
    send = pl.pallas_call(
        up_kernel,
        name="up",
        out_shape=jax.ShapeDtypeStruct((peers, slots + par_count, LANES), F32),
        in_specs=[ANY] * 5,
        out_specs=VMEM,
        scratch_shapes=buffers(*up_args)[:-1] + [pltpu.SemaphoreType.DMA((len(up_args) + 1,))],
        compiler_params=pltpu.CompilerParams(vmem_limit_bytes=UP_MIB * MIB),
        cost_estimate=cost(UP_US),
    )(*up_args)
    recv = lax.all_to_all(send, "leaf", split_axis=0, concat_axis=0, tiled=True)

    picked = pl.pallas_call(
        pick_kernel,
        name="pick",
        out_shape=[jax.ShapeDtypeStruct((leaf_count // 2, 2 * columns, LANES), F32)] * groups,
        in_specs=[VMEM] * 4,
        out_specs=[VMEM] * groups,
        scratch_shapes=[
            pltpu.VMEM((2 * 3 * points // LANES, 2 * columns, LANES), F32),
            pltpu.VMEM(near_list.T.shape, jnp.int32),
            pltpu.SMEM(near_list.T.shape, jnp.int32),
            pltpu.SemaphoreType.DMA((1,)),
        ],
        compiler_params=pltpu.CompilerParams(vmem_limit_bytes=PICK_MIB * MIB),
        cost_estimate=cost(PICK_US),
    )(near_list.T, points_x, left, right)
    parts = [picked[0]] + [
        lax.ppermute(picked[s], "vec", [(i, (i + s) % groups) for i in range(groups)])
        for s in range(1, groups)
    ]

    partial = pl.pallas_call(
        near_kernel,
        name="near",
        out_shape=[jax.ShapeDtypeStruct((columns, points), F32)] * groups,
        in_specs=[ANY] + [VMEM] * groups,
        out_specs=[VMEM] * groups,
        scratch_shapes=buffers(near_blocks),
        compiler_params=pltpu.CompilerParams(vmem_limit_bytes=NEAR_MIB * MIB),
        cost_estimate=cost(NEAR_US),
    )(near_blocks, *parts)
    sums = [partial[0]] + [
        lax.ppermute(partial[s], "vec", [(i, (i - s) % groups) for i in range(groups)])
        for s in range(1, groups)
    ]
    far_args = [
        top_list,
        recv_slot.T,
        top_coupling,
        down_transfer,
        leaf_coupling,
    ]
    fields = pl.pallas_call(
        far_kernel,
        name="far",
        out_shape=jax.ShapeDtypeStruct((par_count, columns * GROUP, LANES), F32),
        in_specs=[VMEM] + [ANY] * len(far_args),
        out_specs=VMEM,
        scratch_shapes=[pltpu.VMEM(array.shape, array.dtype) for array in far_args]
        + [
            pltpu.VMEM((recv_slot.size, peers * slots), BF16),
            pltpu.SemaphoreType.DMA((len(far_args) + par_count,)),
        ],
        compiler_params=pltpu.CompilerParams(vmem_limit_bytes=FAR_MIB * MIB),
        cost_estimate=cost(FAR_US),
    )(recv, *far_args)
    return pl.pallas_call(
        out_kernel,
        name="out",
        out_shape=jax.ShapeDtypeStruct((columns, points), F32),
        in_specs=[VMEM] * (2 + groups),
        out_specs=VMEM,
        compiler_params=pltpu.CompilerParams(vmem_limit_bytes=OUT_MIB * MIB),
        cost_estimate=cost(OUT_US),
    )(fields, out_basis, *sums)


def solution(mesh):
    placed = (
        P("vec", "leaf"),
        P("leaf", None),
        P("vec", None, "leaf"),
        P(None, "leaf"),
        P(None, "leaf"),
        P(None, "leaf"),
        P(None, "leaf"),
        P("leaf", None, None),
        P("leaf", None),
        P("leaf", None),
        P(None, None, "leaf"),
        P("leaf", None),
        P(None, None, "leaf"),
    )
    return jax.shard_map(
        local, mesh=mesh, in_specs=placed, out_specs=P("vec", "leaf"), check_vma=False
    )
```
